512 devices in a mesh: batch: 64 (over y_hi, z, core), tensor: 8 (over y_lo, x).
Axes of the slice: x: 4, y: 4 (y_hi: 2, y_lo: 2; y = y_hi * 2 + y_lo), z: 16, core: 2. Of those that a mesh axis runs over, the one named last changes fastest.
Arguments:
- acts: bfloat16 [8192, 8192], P('batch', 'tensor')
- grads: bfloat16 [8192, 8192], P('batch', 'tensor')
- chosen: int32 [512], replicated, may hold values from 0 to 8191, as said below
- assign: int32 [64], replicated, may hold values from 0 to 63, each once
Outputs:
- scores: float32 [64, 64], P('batch')
The draws below stay inside these ranges and needn't reach their ends.
Inputs may be any that keep to these rules, and one draw needn't show every extreme that they name: `chosen`: distinct values.
All inputs are finite; a program needn't handle non-finite values.
Results may differ from the reference program's by a relative error of at most 0.0003.
Values may be sent and summed in bfloat16 or wider, within the bound.
No kernel may reach another device: no remote copies, remote signals or barrier semaphores. Data moves between devices by JAX's collectives and lax.ppermute only.
A program may use at most 64 MiB of HBM per device.

```python
import jax
import jax.numpy as jnp
from jax import lax

D = 8192
NSEL = 512
TOK = 128
NSEQ = 64


def token_kinds(key):
    return jax.random.randint(jax.random.fold_in(key, 5), (NSEQ * TOK,), 0, TOK).astype(jnp.int32)


def draw_acts(key, part):
    kinds = token_kinds(key)
    key = jax.random.fold_in(key, 11)
    row_total = NSEQ * TOK
    pool = jax.random.normal(jax.random.fold_in(key, 1), (TOK, D), jnp.float32)
    noise = jax.random.normal(jax.random.fold_in(key, 2), (row_total, D), jnp.float32)
    return (pool[kinds] + 0.5 * noise).astype(jnp.bfloat16)


def draw_grads(key, part):
    kinds = token_kinds(key)
    key = jax.random.fold_in(key, 23)
    row_total = NSEQ * TOK
    pool = jax.random.normal(jax.random.fold_in(key, 1), (TOK, D), jnp.float32)
    noise = jax.random.normal(jax.random.fold_in(key, 2), (row_total, D), jnp.float32)
    return (pool[kinds] + 0.5 * noise).astype(jnp.bfloat16)


def draw_chosen(key, part):
    key = jax.random.fold_in(key, 37)
    middle = jax.random.permutation(key, D - 2).astype(jnp.int32) + 1
    ends = jnp.array([0, D - 1], jnp.int32)
    return jnp.concatenate([ends, middle[:NSEL - 2]])


def setup_inputs(seed: int = 0) -> dict:
    splits = jax.random.split(jax.random.key(seed), 5)
    return {
        "acts": draw_acts(jax.random.fold_in(splits[4], 71), 0),
        "grads": draw_grads(jax.random.fold_in(splits[4], 71), 0),
        "chosen": draw_chosen(jax.random.fold_in(splits[4], 71), 0),
        "assign": jax.random.permutation(splits[3], NSEQ).astype(jnp.int32),
    }


def reference(acts, grads, chosen, assign):
    picked = jnp.take(grads, chosen, axis=1)
    seq_acts = acts.reshape(NSEQ, TOK, D)
    seq_grads = picked.reshape(NSEQ, TOK, NSEL)
    contract_dims = (((1,), (1,)), ((), ()))

    def row_block(row_pair):
        left_acts, left_grads = row_pair
        feat_gram = lax.dot_general(left_acts, acts, contract_dims, preferred_element_type=jnp.float32)
        grad_gram = lax.dot_general(left_grads, picked, contract_dims, preferred_element_type=jnp.float32)
        return (feat_gram * grad_gram).reshape(TOK, NSEQ, TOK).sum(axis=(0, 2))

    inner = lax.map(row_block, (seq_acts, seq_grads))
    norming = 1.0 / (float(TOK) * float(D) * float(NSEL))
    return jnp.zeros((NSEQ, NSEQ), jnp.float32).at[:, assign].set(inner * norming)
```

```python
import jax
import jax.numpy as jnp
from jax import lax
from jax.sharding import PartitionSpec as P

D = 8192
NSEL = 512
TOK = 128


def summed_over_tensor(part):
    group = lax.axis_size("tensor")
    rows = part.shape[0] // group
    shares = lax.all_to_all(
        part.reshape(group, rows, part.shape[1]), "tensor", 0, 0, tiled=True
    )
    own = shares.astype(jnp.float32).sum(axis=0).astype(part.dtype)
    copies = jnp.broadcast_to(own[None], (group, rows, part.shape[1]))
    return lax.all_to_all(copies, "tensor", 0, 0, tiled=True).reshape(part.shape)


def on_device(acts, grads, chosen, assign):
    width = grads.shape[1]
    cycle_size = lax.axis_size("batch")
    group = lax.axis_size("tensor")
    local = chosen - lax.axis_index("tensor") * width
    places = lax.broadcasted_iota(jnp.int32, (width, NSEL), 0)
    selector = (places == local[None, :]).astype(grads.dtype)
    part = lax.dot_general(
        grads, selector, (((1,), (0,)), ((), ())), preferred_element_type=jnp.float32
    ).astype(grads.dtype)
    picked = summed_over_tensor(part)

    example_grad = lax.dot_general(
        acts, picked, (((0,), (0,)), ((), ())), preferred_element_type=jnp.float32
    ).astype(acts.dtype)
    shares = lax.all_to_all(
        example_grad.reshape(cycle_size, width // cycle_size, NSEL), "batch", 0, 0, tiled=True
    )
    pairs = lax.dot_general(
        shares, shares, (((1, 2), (1, 2)), ((), ())), preferred_element_type=jnp.float32
    )
    rows = lax.all_to_all(pairs[:, None, :], "batch", 0, 0, tiled=True).sum(axis=0)
    rows = jnp.broadcast_to(rows[None], (group, 1, cycle_size))
    row = lax.all_to_all(rows, "tensor", 0, 0, tiled=True).sum(axis=0)
    norming = 1.0 / (float(TOK) * float(D) * float(NSEL))
    slots = lax.broadcasted_iota(jnp.int32, (cycle_size, cycle_size), 0)
    placed = jnp.where(slots == assign[None, :], row * norming, 0.0)
    return placed.sum(axis=1)[None]


def solution(mesh):
    placed = (P("batch", "tensor"), P("batch", "tensor"), P(), P())
    return jax.shard_map(
        on_device, mesh=mesh, in_specs=placed, out_specs=P("batch", None), check_vma=False
    )
```

```python
import jax
import jax.numpy as jnp
from jax import lax
from jax.experimental import pallas as pl
from jax.experimental.pallas import tpu as pltpu
from jax.sharding import PartitionSpec as P

D = 8192
NSEL = 512
TOK = 128
Y_HI, QUARTERS, RUN, CORES = 2, 4, 4, 2
SIDES = Y_HI * CORES
MEMBERS = RUN * SIDES
TENSOR = 8
WIDTH = D // TENSOR
PART = WIDTH // QUARTERS
ROWS = PART // MEMBERS
TROWS = TOK // TENSOR


def batch_index(y_hi, quarter, place, core):
    return ((y_hi * QUARTERS + quarter) * RUN + place) * CORES + core


def to_quarter(block, distance):
    route = [
        (batch_index(y, q, r, c), batch_index(y, (q + distance) % QUARTERS, r, c))
        for y in range(Y_HI)
        for q in range(QUARTERS)
        for r in range(RUN)
        for c in range(CORES)
    ]
    return lax.ppermute(block, "batch", route)


def run_groups():
    return [
        [batch_index(y, q, r, c) for r in range(RUN) for y in range(Y_HI) for c in range(CORES)]
        for q in range(QUARTERS)
    ]


def column_groups():
    return [
        [batch_index(y, q, r, c) for q in range(QUARTERS) for r in range(RUN)]
        for y in range(Y_HI)
        for c in range(CORES)
    ]


def plane_groups():
    return [
        [
            batch_index(y, q, r, c) * TENSOR + t
            for y in range(Y_HI)
            for c in range(CORES)
            for t in range(TENSOR)
        ]
        for q in range(QUARTERS)
        for r in range(RUN)
    ]


def example_grads_kernel(quarter_ref, acts_ref, first_ref, second_ref, third_ref, picked_ref, out_ref):
    quarter = quarter_ref[0]
    for distance in range(QUARTERS):
        if distance == 0:
            acts = acts_ref[:, pl.ds(pl.multiple_of(quarter * PART, PART), PART)]
        else:
            acts = (first_ref, second_ref, third_ref)[distance - 1][...]
        picked = picked_ref[:, distance].reshape(TOK, NSEL)
        grad = lax.dot_general(
            acts, picked, (((0,), (0,)), ((), ())), preferred_element_type=jnp.float32
        ).astype(out_ref.dtype)
        origin = lax.rem(quarter + QUARTERS - distance, QUARTERS)
        out_ref[:, pl.ds(origin, 1)] = grad.reshape(MEMBERS, 1, ROWS, NSEL)


def example_grads(quarter, acts, others, picked):
    smem = pl.BlockSpec(memory_space=pltpu.SMEM)
    vmem = pl.BlockSpec(memory_space=pltpu.VMEM)
    return pl.pallas_call(
        example_grads_kernel,
        out_shape=jax.ShapeDtypeStruct((MEMBERS, QUARTERS, ROWS, NSEL), acts.dtype),
        in_specs=[smem] + [vmem] * 5,
        out_specs=vmem,
        compiler_params=pltpu.CompilerParams(vmem_limit_bytes=16 * 1024 * 1024),
        cost_estimate=pl.CostEstimate(
            flops=2 * QUARTERS * PART * TOK * NSEL, bytes_accessed=2 * 1024 * 1024, transcendentals=0
        ),
    )(quarter[None], acts, *others, picked)


def on_device(acts, grads, chosen, assign):
    quarter = lax.rem(lax.axis_index("batch") // (RUN * CORES), QUARTERS)
    local = chosen - lax.axis_index("tensor") * WIDTH
    places = lax.broadcasted_iota(jnp.int32, (WIDTH, NSEL), 0)
    selector = (places == local[None, :]).astype(grads.dtype)
    part = lax.dot_general(
        grads, selector, (((1,), (0,)), ((), ())), preferred_element_type=jnp.float32
    ).astype(grads.dtype)
    shares = lax.all_to_all(part.reshape(TENSOR, TROWS, NSEL), "tensor", 0, 0, tiled=True)
    own = shares.astype(jnp.float32).sum(axis=0).astype(part.dtype)

    chunks = [own] + [to_quarter(own, distance) for distance in range(1, QUARTERS)]
    others = []
    for distance in range(1, QUARTERS):
        there = lax.rem(quarter + distance, QUARTERS)
        others.append(to_quarter(lax.dynamic_slice(acts, (0, there * PART), (TOK, PART)), distance))
    copies = jnp.broadcast_to(jnp.stack(chunks)[None], (TENSOR, QUARTERS, TROWS, NSEL))
    picked = lax.all_to_all(copies, "tensor", 0, 0, tiled=True)

    terms = example_grads(quarter, acts, others, picked)
    terms = lax.all_to_all(terms, "batch", 0, 0, axis_index_groups=run_groups(), tiled=True)
    terms = terms.reshape(MEMBERS * QUARTERS, ROWS, NSEL)
    pairs = lax.dot_general(
        terms, terms, (((1, 2), (1, 2)), ((), ())), preferred_element_type=jnp.float32
    )
    rows = pairs.reshape(RUN, SIDES, QUARTERS, RUN * SIDES * QUARTERS)
    rows = jnp.transpose(rows, (2, 0, 1, 3)).reshape(QUARTERS * RUN, SIDES, RUN * SIDES * QUARTERS)
    rows = lax.all_to_all(rows, "batch", 0, 0, axis_index_groups=column_groups(), tiled=True).sum(axis=0)
    rows = jnp.broadcast_to(rows[:, None], (SIDES, TENSOR, rows.shape[1]))
    rows = rows.reshape(SIDES * TENSOR, 1, rows.shape[2])
    row = lax.all_to_all(
        rows, ("batch", "tensor"), 0, 0, axis_index_groups=plane_groups(), tiled=True
    ).sum(axis=(0, 1))

    ids = assign.reshape(Y_HI, QUARTERS, RUN, CORES)
    ids = jnp.transpose(ids, (2, 0, 3, 1)).reshape(-1)
    norming = 1.0 / (float(TOK) * float(D) * float(NSEL))
    slots = lax.broadcasted_iota(jnp.int32, (ids.shape[0], ids.shape[0]), 0)
    placed = jnp.where(slots == ids[None, :], row * norming, 0.0)
    return placed.sum(axis=1)[None]


def solution(mesh):
    placed = (P("batch", "tensor"), P("batch", "tensor"), P(), P())
    return jax.shard_map(
        on_device, mesh=mesh, in_specs=placed, out_specs=P("batch", None), check_vma=False
    )
```

```python
import jax
import jax.numpy as jnp
from jax import lax
from jax.experimental import pallas as pl
from jax.experimental.pallas import tpu as pltpu
from jax.sharding import PartitionSpec as P

D = 8192
NSEL = 512
TOK = 128
Y_HI, PAIRS, PLACES, CORES = 2, 8, 2, 2
SEQS = Y_HI * PAIRS * PLACES * CORES
MEMBERS = PLACES * Y_HI * CORES
Y_LO, X = 2, 4
TENSOR = Y_LO * X
WIDTH = D // TENSOR
PART = WIDTH // PAIRS
HALF = NSEL // Y_LO
TROWS = TOK // X
LANES = 128
BLOCKS = HALF // LANES
PIECE = BLOCKS * TROWS
ROWS = PART * Y_LO // MEMBERS


def batch_index(y_hi, pair, place, core):
    return ((y_hi * PAIRS + pair) * PLACES + place) * CORES + core


def column_groups():
    return [
        [batch_index(y, k, r, c) for k in range(PAIRS)]
        for y in range(Y_HI)
        for r in range(PLACES)
        for c in range(CORES)
    ]


def pair_groups():
    return [
        [batch_index(y, k, r, c) for r in range(PLACES) for y in range(Y_HI) for c in range(CORES)]
        for k in range(PAIRS)
    ]


def whole_group():
    return [
        [
            batch_index(y, k, r, c)
            for r in range(PLACES)
            for y in range(Y_HI)
            for c in range(CORES)
            for k in range(PAIRS)
        ]
    ]


def x_groups():
    return [[y * X + x for x in range(X)] for y in range(Y_LO)]


def select_kernel(index_ref, chosen_ref, grads_ref, out_ref):
    local = chosen_ref[...] - index_ref[0] * WIDTH
    places = lax.broadcasted_iota(jnp.int32, (WIDTH, NSEL), 0)
    selector = jnp.where(places == local, 1.0, 0.0).astype(grads_ref.dtype)
    part = jnp.dot(grads_ref[...], selector, preferred_element_type=jnp.float32)
    part = part.astype(out_ref.dtype)
    for y in range(Y_LO):
        for j in range(BLOCKS):
            lane = (y * BLOCKS + j) * LANES
            block = part[:, lane : lane + LANES].reshape(X, TROWS, LANES)
            out_ref[y * X : (y + 1) * X, j * TROWS : (j + 1) * TROWS] = block


def selected(index, chosen, grads):
    vmem = pl.BlockSpec(memory_space=pltpu.VMEM)
    return pl.pallas_call(
        select_kernel,
        out_shape=jax.ShapeDtypeStruct((TENSOR, PIECE, LANES), grads.dtype),
        in_specs=[pl.BlockSpec(memory_space=pltpu.SMEM), vmem, vmem],
        out_specs=vmem,
        compiler_params=pltpu.CompilerParams(vmem_limit_bytes=16 * 1024 * 1024),
    )(index[None], chosen[None], grads)


def pack_kernel(acts_ref, shares_ref, out_ref):
    piece = shares_ref[0].astype(jnp.float32)
    for t in range(1, TENSOR):
        piece = piece + shares_ref[t].astype(jnp.float32)
    piece = piece.astype(out_ref.dtype)
    for k in range(PAIRS):
        out_ref[k, :TOK] = acts_ref[:, k * PART : (k + 1) * PART]
        out_ref[k, TOK:] = piece


def packed(acts, shares):
    vmem = pl.BlockSpec(memory_space=pltpu.VMEM)
    return pl.pallas_call(
        pack_kernel,
        out_shape=jax.ShapeDtypeStruct((PAIRS, TOK + PIECE, LANES), acts.dtype),
        in_specs=[vmem, vmem],
        out_specs=vmem,
        compiler_params=pltpu.CompilerParams(vmem_limit_bytes=16 * 1024 * 1024),
    )(acts, shares)


def example_grads_kernel(own_ref, other_ref, picked_ref, out_ref):
    count = PART // ROWS
    for k in range(PAIRS):
        blocks = [
            picked_ref[:, k, j * TROWS : (j + 1) * TROWS].reshape(TOK, LANES) for j in range(BLOCKS)
        ]
        picked = jnp.concatenate(blocks, axis=1)
        for side, ref in enumerate((own_ref, other_ref)):
            grad = lax.dot_general(
                ref[k, :TOK], picked, (((0,), (0,)), ((), ())), preferred_element_type=jnp.float32
            ).astype(out_ref.dtype)
            out_ref[side * count : (side + 1) * count, k] = grad.reshape(count, ROWS, HALF)


def example_grads(own, other, picked):
    vmem = pl.BlockSpec(memory_space=pltpu.VMEM)
    return pl.pallas_call(
        example_grads_kernel,
        out_shape=jax.ShapeDtypeStruct((MEMBERS, PAIRS, ROWS, HALF), own.dtype),
        in_specs=[vmem] * 3,
        out_specs=vmem,
        compiler_params=pltpu.CompilerParams(vmem_limit_bytes=16 * 1024 * 1024),
        cost_estimate=pl.CostEstimate(
            flops=4 * PAIRS * PART * TOK * HALF, bytes_accessed=2 * 1024 * 1024, transcendentals=0
        ),
    )(own, other, picked)


def on_device(acts, grads, chosen, assign):
    part = selected(lax.axis_index("tensor"), chosen, grads)
    shares = lax.all_to_all(part, "tensor", 0, 0, tiled=True)
    both = lax.all_to_all(
        packed(acts, shares), "batch", 0, 0, axis_index_groups=column_groups(), tiled=True
    )
    copies = jnp.broadcast_to(both[None, :, TOK:], (X, PAIRS, PIECE, LANES))
    picked = lax.all_to_all(copies, "tensor", 0, 0, axis_index_groups=x_groups(), tiled=True)
    other = lax.ppermute(both[:, :TOK], "tensor", [(t, (t + X) % TENSOR) for t in range(TENSOR)])

    terms = example_grads(both, other, picked)
    terms = lax.all_to_all(terms, "batch", 0, 0, axis_index_groups=pair_groups(), tiled=True)
    terms = terms.reshape(SEQS, ROWS, HALF)
    pairs = lax.dot_general(
        terms, terms, (((1, 2), (1, 2)), ((), ())), preferred_element_type=jnp.float32
    )
    rows = lax.all_to_all(
        pairs[:, None, :], "batch", 0, 0, axis_index_groups=whole_group(), tiled=True
    ).sum(axis=0)
    rows = jnp.broadcast_to(rows[None], (TENSOR, 1, SEQS))
    row = lax.all_to_all(rows, "tensor", 0, 0, tiled=True).sum(axis=0)
    ids = assign.reshape(Y_HI, PAIRS, PLACES, CORES)
    ids = jnp.transpose(ids, (2, 0, 3, 1)).reshape(-1)
    norming = 1.0 / (float(TOK) * float(D) * float(NSEL))
    slots = lax.broadcasted_iota(jnp.int32, (SEQS, SEQS), 0)
    placed = jnp.where(slots == ids[None, :], row * norming, 0.0)
    return placed.sum(axis=1)[None]


def solution(mesh):
    placed = (P("batch", "tensor"), P("batch", "tensor"), P(), P())
    return jax.shard_map(
        on_device, mesh=mesh, in_specs=placed, out_specs=P("batch", None), check_vma=False
    )
```

```python
import jax
import jax.numpy as jnp
from jax import lax
from jax.experimental import pallas as pl
from jax.experimental.pallas import tpu as pltpu
from jax.sharding import PartitionSpec as P

D = 8192
NSEL = 512
TOK = 128
Y_HI, PAIRS, PLACES, CORES = 2, 8, 2, 2
SEQS = Y_HI * PAIRS * PLACES * CORES
SIDES = Y_HI * CORES
DEPTH = PAIRS * PLACES
MEMBERS = PLACES * SIDES
Y_LO, X = 2, 4
TENSOR = Y_LO * X
WIDTH = D // TENSOR
PART = WIDTH // PAIRS
HALF = NSEL // Y_LO
TROWS = TOK // X
LANES = 128
BLOCKS = HALF // LANES
PIECE = BLOCKS * TROWS
ROWS = PART * Y_LO // MEMBERS


def batch_index(y_hi, pair, place, core):
    return ((y_hi * PAIRS + pair) * PLACES + place) * CORES + core


def column_groups():
    return [
        [batch_index(y, k, r, c) for k in range(PAIRS)]
        for y in range(Y_HI)
        for r in range(PLACES)
        for c in range(CORES)
    ]


def pair_groups():
    return [
        [batch_index(y, k, r, c) for r in range(PLACES) for y in range(Y_HI) for c in range(CORES)]
        for k in range(PAIRS)
    ]


def depth_groups():
    return [
        [batch_index(y, k, r, c) for k in range(PAIRS) for r in range(PLACES)]
        for y in range(Y_HI)
        for c in range(CORES)
    ]


def plane_groups():
    return [
        [
            batch_index(y, k, r, c) * TENSOR + t
            for y in range(Y_HI)
            for c in range(CORES)
            for t in range(TENSOR)
        ]
        for k in range(PAIRS)
        for r in range(PLACES)
    ]


def x_groups():
    return [[y * X + x for x in range(X)] for y in range(Y_LO)]


def kernel_call(kernel, out_shape, in_specs, args, scratch=(), limit=24 * 1024 * 1024):
    vmem = pl.BlockSpec(memory_space=pltpu.VMEM)
    return pl.pallas_call(
        kernel,
        out_shape=out_shape,
        in_specs=[vmem] * len(args) if in_specs is None else in_specs,
        out_specs=jax.tree.map(lambda _: vmem, out_shape),
        scratch_shapes=scratch,
        compiler_params=pltpu.CompilerParams(vmem_limit_bytes=limit),
    )(*args)


def select_kernel(index_ref, chosen_hbm, grads_hbm, out_ref, chosen_ref, grads_ref, sems):
    first = pltpu.make_async_copy(chosen_hbm, chosen_ref, sems.at[0])
    second = pltpu.make_async_copy(grads_hbm, grads_ref, sems.at[1])
    first.start()
    second.start()
    first.wait()
    local = chosen_ref[...] - index_ref[0] * WIDTH
    places = lax.broadcasted_iota(jnp.int32, (WIDTH, NSEL), 0)
    selector = jnp.where(places == local, 1.0, 0.0).astype(grads_ref.dtype)
    second.wait()
    part = jnp.dot(grads_ref[...], selector, preferred_element_type=jnp.float32)
    part = part.astype(out_ref.dtype)
    for y in range(Y_LO):
        for j in range(BLOCKS):
            lane = (y * BLOCKS + j) * LANES
            block = part[:, lane : lane + LANES].reshape(X, TROWS, LANES)
            out_ref[y * X : (y + 1) * X, j * TROWS : (j + 1) * TROWS] = block


def selected(index, chosen, grads):
    hbm = pl.BlockSpec(memory_space=pltpu.HBM)
    return kernel_call(
        select_kernel,
        jax.ShapeDtypeStruct((TENSOR, PIECE, LANES), grads.dtype),
        [pl.BlockSpec(memory_space=pltpu.SMEM), hbm, hbm],
        (index[None], chosen[None], grads),
        [
            pltpu.VMEM((1, NSEL), jnp.int32),
            pltpu.VMEM((TOK, WIDTH), grads.dtype),
            pltpu.SemaphoreType.DMA((2,)),
        ],
        None,
    )


def pack_kernel(acts_ref, shares_ref, out_ref):
    piece = shares_ref[0].astype(jnp.float32)
    for t in range(1, TENSOR):
        piece = piece + shares_ref[t].astype(jnp.float32)
    piece = piece.astype(out_ref.dtype)
    for k in range(PAIRS):
        out_ref[k, :TOK] = acts_ref[:, k * PART : (k + 1) * PART]
        out_ref[k, TOK:] = piece


def packed(acts, shares):
    shape = jax.ShapeDtypeStruct((PAIRS, TOK + PIECE, LANES), acts.dtype)
    return kernel_call(pack_kernel, shape, None, (acts, shares))


def unpack_kernel(both_ref, own_ref, copies_ref):
    own_ref[...] = both_ref[:, :TOK]
    for x in range(X):
        copies_ref[x] = both_ref[:, TOK:]


def unpacked(both):
    shapes = (
        jax.ShapeDtypeStruct((PAIRS, TOK, PART), both.dtype),
        jax.ShapeDtypeStruct((X, PAIRS, PIECE, LANES), both.dtype),
    )
    return kernel_call(unpack_kernel, shapes, None, (both,))


def example_grads_kernel(own_ref, other_ref, picked_ref, out_ref):
    count = PART // ROWS
    for k in range(PAIRS):
        blocks = [
            picked_ref[:, k, j * TROWS : (j + 1) * TROWS].reshape(TOK, LANES) for j in range(BLOCKS)
        ]
        picked = jnp.concatenate(blocks, axis=1)
        for side, ref in enumerate((own_ref, other_ref)):
            grad = lax.dot_general(
                ref[k], picked, (((0,), (0,)), ((), ())), preferred_element_type=jnp.float32
            ).astype(out_ref.dtype)
            out_ref[side * count : (side + 1) * count, k] = grad.reshape(count, ROWS, HALF)


def example_grads(own, other, picked):
    shape = jax.ShapeDtypeStruct((MEMBERS, PAIRS, ROWS, HALF), own.dtype)
    return kernel_call(example_grads_kernel, shape, None, (own, other, picked))


def pairs_kernel(terms_ref, out_ref, *wide_refs):
    wide = terms_ref[...].reshape(SEQS * ROWS, HALF).astype(jnp.float32)
    for j, wide_ref in enumerate(wide_refs):
        wide_ref[...] = wide[:, j * LANES : (j + 1) * LANES]
    total = jnp.zeros((SEQS, SEQS), jnp.float32)
    group = 4
    for first in range(0, ROWS, group):
        rows = [
            wide_ref[pl.ds(f, SEQS, stride=ROWS), :]
            for f in range(first, first + group)
            for wide_ref in wide_refs
        ]
        rows = jnp.concatenate(rows, axis=1).astype(terms_ref.dtype)
        total += lax.dot_general(
            rows, rows, (((1,), (1,)), ((), ())), preferred_element_type=jnp.float32
        )
    for r in range(PLACES):
        sides = [
            total[(r * SIDES + q) * PAIRS : (r * SIDES + q + 1) * PAIRS] for q in range(SIDES)
        ]
        out_ref[:, r, 0] = jnp.concatenate(sides, axis=1)


def pairs(terms):
    return kernel_call(
        pairs_kernel,
        jax.ShapeDtypeStruct((PAIRS, PLACES, 1, SIDES * SEQS), jnp.float32),
        None,
        (terms,),
        [pltpu.VMEM((SEQS * ROWS, LANES), jnp.float32)] * BLOCKS,
    )


def side_kernel(rows_ref, out_ref):
    sums = rows_ref[0]
    for z in range(1, DEPTH):
        sums = sums + rows_ref[z]
    for q in range(SIDES):
        out_ref[q] = jnp.broadcast_to(sums[:, q * SEQS : (q + 1) * SEQS][None], (TENSOR, 1, SEQS))


def place_kernel(rows_ref, ids_ref, out_ref):
    row = rows_ref[0]
    for member in range(1, SIDES * TENSOR):
        row = row + rows_ref[member]
    slots = lax.broadcasted_iota(jnp.int32, (SEQS, SEQS), 0)
    spots = jnp.where(slots == ids_ref[...], 1.0, 0.0)
    norming = 1.0 / (float(TOK) * float(D) * float(NSEL))
    out_ref[...] = lax.dot_general(
        row * norming,
        spots,
        (((1,), (1,)), ((), ())),
        precision=lax.Precision.HIGHEST,
        preferred_element_type=jnp.float32,
    )


def on_device(acts, grads, chosen, assign):
    part = selected(lax.axis_index("tensor"), chosen, grads)
    shares = lax.all_to_all(part, "tensor", 0, 0, tiled=True)
    both = lax.all_to_all(
        packed(acts, shares), "batch", 0, 0, axis_index_groups=column_groups(), tiled=True
    )
    own, copies = unpacked(both)
    picked = lax.all_to_all(copies, "tensor", 0, 0, axis_index_groups=x_groups(), tiled=True)
    other = lax.ppermute(own, "tensor", [(t, (t + X) % TENSOR) for t in range(TENSOR)])

    terms = example_grads(own, other, picked)
    terms = lax.all_to_all(terms, "batch", 0, 0, axis_index_groups=pair_groups(), tiled=True)
    rows = pairs(terms).reshape(DEPTH, 1, SIDES * SEQS)
    rows = lax.all_to_all(rows, "batch", 0, 0, axis_index_groups=depth_groups(), tiled=True)
    shape = jax.ShapeDtypeStruct((SIDES, TENSOR, 1, SEQS), jnp.float32)
    rows = kernel_call(side_kernel, shape, None, (rows,)).reshape(SIDES * TENSOR, 1, SEQS)
    rows = lax.all_to_all(
        rows, ("batch", "tensor"), 0, 0, axis_index_groups=plane_groups(), tiled=True
    )
    ids = assign.reshape(Y_HI, PAIRS, PLACES, CORES)
    ids = jnp.transpose(ids, (2, 0, 3, 1)).reshape(1, SEQS)
    shape = jax.ShapeDtypeStruct((1, SEQS), jnp.float32)
    return kernel_call(place_kernel, shape, None, (rows, ids))


def solution(mesh):
    placed = (P("batch", "tensor"), P("batch", "tensor"), P(), P())
    return jax.shard_map(
        on_device, mesh=mesh, in_specs=placed, out_specs=P("batch", None), check_vma=False
    )
```

```python
import jax
import jax.numpy as jnp
from jax import lax
from jax.experimental import pallas as pl
from jax.experimental.pallas import tpu as pltpu
from jax.sharding import PartitionSpec as P

D = 8192
NSEL = 512
TOK = 128
Y_HI, PAIRS, PLACES, CORES = 2, 8, 2, 2
SEQS = Y_HI * PAIRS * PLACES * CORES
SIDES = Y_HI * CORES
DEPTH = PAIRS * PLACES
MEMBERS = PLACES * SIDES
Y_LO, X = 2, 4
TENSOR = Y_LO * X
WIDTH = D // TENSOR
PART = WIDTH // PAIRS
HALF = NSEL // Y_LO
TROWS = TOK // X
LANES = 128
BLOCKS = HALF // LANES
PIECE = BLOCKS * TROWS
ROWS = PART * Y_LO // MEMBERS


def batch_index(y_hi, pair, place, core):
    return ((y_hi * PAIRS + pair) * PLACES + place) * CORES + core


def column_groups():
    return [
        [batch_index(y, k, r, c) for k in range(PAIRS)]
        for y in range(Y_HI)
        for r in range(PLACES)
        for c in range(CORES)
    ]


def pair_groups():
    return [
        [batch_index(y, k, r, c) for r in range(PLACES) for y in range(Y_HI) for c in range(CORES)]
        for k in range(PAIRS)
    ]


def depth_groups():
    return [
        [batch_index(y, k, r, c) for k in range(PAIRS) for r in range(PLACES)]
        for y in range(Y_HI)
        for c in range(CORES)
    ]


def plane_groups():
    return [
        [
            batch_index(y, k, r, c) * TENSOR + t
            for y in range(Y_HI)
            for c in range(CORES)
            for t in range(TENSOR)
        ]
        for k in range(PAIRS)
        for r in range(PLACES)
    ]


def x_groups():
    return [[y * X + x for x in range(X)] for y in range(Y_LO)]


def kernel_call(kernel, out_shape, args):
    vmem = pl.BlockSpec(memory_space=pltpu.VMEM)
    return pl.pallas_call(
        kernel,
        out_shape=out_shape,
        in_specs=[vmem] * len(args),
        out_specs=jax.tree.map(lambda _: vmem, out_shape),
        compiler_params=pltpu.CompilerParams(vmem_limit_bytes=24 * 1024 * 1024),
    )(*args)


def select_kernel(local_ref, grads_ref, out_ref):
    places = lax.broadcasted_iota(jnp.int32, (WIDTH, NSEL), 0)
    selector = jnp.where(places == local_ref[...], 1.0, 0.0).astype(grads_ref.dtype)
    part = jnp.dot(grads_ref[...], selector, preferred_element_type=jnp.float32)
    part = part.astype(out_ref.dtype)
    for y in range(Y_LO):
        for j in range(BLOCKS):
            lane = (y * BLOCKS + j) * LANES
            block = part[:, lane : lane + LANES].reshape(X, TROWS, LANES)
            out_ref[y * X : (y + 1) * X, j * TROWS : (j + 1) * TROWS] = block


def selected(chosen, grads):
    local = (chosen - lax.axis_index("tensor") * WIDTH)[None]
    shape = jax.ShapeDtypeStruct((TENSOR, PIECE, LANES), grads.dtype)
    return kernel_call(select_kernel, shape, (local, grads))


def pack_kernel(acts_ref, shares_ref, out_ref):
    piece = shares_ref[0].astype(jnp.float32)
    for t in range(1, TENSOR):
        piece = piece + shares_ref[t].astype(jnp.float32)
    piece = piece.astype(out_ref.dtype)
    for k in range(PAIRS):
        out_ref[k, :TOK] = acts_ref[:, k * PART : (k + 1) * PART]
        out_ref[k, TOK:] = piece


def packed(acts, shares):
    shape = jax.ShapeDtypeStruct((PAIRS, TOK + PIECE, LANES), acts.dtype)
    return kernel_call(pack_kernel, shape, (acts, shares))


def unpack_kernel(both_ref, own_ref, copies_ref):
    own_ref[...] = both_ref[:, :TOK]
    for x in range(X):
        copies_ref[x] = both_ref[:, TOK:]


def unpacked(both):
    shapes = (
        jax.ShapeDtypeStruct((PAIRS, TOK, PART), both.dtype),
        jax.ShapeDtypeStruct((X, PAIRS, PIECE, LANES), both.dtype),
    )
    return kernel_call(unpack_kernel, shapes, (both,))


def example_grads_kernel(own_ref, other_ref, picked_ref, assign_ref, out_ref, spots_ref):
    count = PART // ROWS
    for k in range(PAIRS):
        blocks = [
            picked_ref[:, k, j * TROWS : (j + 1) * TROWS].reshape(TOK, LANES) for j in range(BLOCKS)
        ]
        picked = jnp.concatenate(blocks, axis=1)
        for side, ref in enumerate((own_ref, other_ref)):
            grad = lax.dot_general(
                ref[k], picked, (((0,), (0,)), ((), ())), preferred_element_type=jnp.float32
            ).astype(out_ref.dtype)
            out_ref[side * count : (side + 1) * count, k] = grad.reshape(count, ROWS, HALF)
    column = lax.broadcasted_iota(jnp.int32, (SEQS, SEQS), 0)
    slot = lax.broadcasted_iota(jnp.int32, (SEQS, SEQS), 1)
    pair, core = column % PAIRS, column // PAIRS % CORES
    y_hi, place = column // (PAIRS * CORES) % Y_HI, column // (PAIRS * SIDES)
    ordered = jnp.where(batch_index(y_hi, pair, place, core) == slot, 1.0, 0.0)
    wanted = jnp.where(column == assign_ref[...], 1.0, 0.0)
    spots_ref[...] = lax.dot_general(
        ordered, wanted, (((1,), (1,)), ((), ())), preferred_element_type=jnp.float32
    )


def example_grads(own, other, picked, assign):
    shapes = (
        jax.ShapeDtypeStruct((MEMBERS, PAIRS, ROWS, HALF), own.dtype),
        jax.ShapeDtypeStruct((SEQS, SEQS), jnp.float32),
    )
    return kernel_call(example_grads_kernel, shapes, (own, other, picked, assign[None]))


def pairs_kernel(terms_ref, out_ref):
    terms = jnp.swapaxes(terms_ref[...].reshape(SEQS, ROWS, HALF), 0, 1)
    total = jnp.zeros((SEQS, SEQS), jnp.float32)
    for row in range(ROWS):
        total += lax.dot_general(
            terms[row], terms[row], (((1,), (1,)), ((), ())), preferred_element_type=jnp.float32
        )
    for r in range(PLACES):
        sides = [
            total[(r * SIDES + q) * PAIRS : (r * SIDES + q + 1) * PAIRS] for q in range(SIDES)
        ]
        out_ref[:, r, 0] = jnp.concatenate(sides, axis=1)


def pairs(terms):
    shape = jax.ShapeDtypeStruct((PAIRS, PLACES, 1, SIDES * SEQS), jnp.float32)
    return kernel_call(pairs_kernel, shape, (terms,))


def side_kernel(rows_ref, out_ref):
    sums = rows_ref[0]
    for z in range(1, DEPTH):
        sums = sums + rows_ref[z]
    for q in range(SIDES):
        out_ref[q] = jnp.broadcast_to(sums[:, q * SEQS : (q + 1) * SEQS][None], (TENSOR, 1, SEQS))


def place_kernel(rows_ref, spots_ref, out_ref):
    row = rows_ref[0]
    for member in range(1, SIDES * TENSOR):
        row = row + rows_ref[member]
    norming = 1.0 / (float(TOK) * float(D) * float(NSEL))
    out_ref[...] = lax.dot_general(
        row * norming,
        spots_ref[...],
        (((1,), (0,)), ((), ())),
        precision=lax.Precision.HIGHEST,
        preferred_element_type=jnp.float32,
    )


def on_device(acts, grads, chosen, assign):
    part = selected(chosen, grads)
    shares = lax.all_to_all(part, "tensor", 0, 0, tiled=True)
    both = lax.all_to_all(
        packed(acts, shares), "batch", 0, 0, axis_index_groups=column_groups(), tiled=True
    )
    own, copies = unpacked(both)
    picked = lax.all_to_all(copies, "tensor", 0, 0, axis_index_groups=x_groups(), tiled=True)
    other = lax.ppermute(own, "tensor", [(t, (t + X) % TENSOR) for t in range(TENSOR)])

    terms, spots = example_grads(own, other, picked, assign)
    terms = lax.all_to_all(terms, "batch", 0, 0, axis_index_groups=pair_groups(), tiled=True)
    rows = pairs(terms).reshape(DEPTH, 1, SIDES * SEQS)
    rows = lax.all_to_all(rows, "batch", 0, 0, axis_index_groups=depth_groups(), tiled=True)
    shape = jax.ShapeDtypeStruct((SIDES, TENSOR, 1, SEQS), jnp.float32)
    rows = kernel_call(side_kernel, shape, (rows,)).reshape(SIDES * TENSOR, 1, SEQS)
    rows = lax.all_to_all(
        rows, ("batch", "tensor"), 0, 0, axis_index_groups=plane_groups(), tiled=True
    )
    shape = jax.ShapeDtypeStruct((1, SEQS), jnp.float32)
    return kernel_call(place_kernel, shape, (rows, spots))


def solution(mesh):
    placed = (P("batch", "tensor"), P("batch", "tensor"), P(), P())
    return jax.shard_map(
        on_device, mesh=mesh, in_specs=placed, out_specs=P("batch", None), check_vma=False
    )
```

```python
import jax
import jax.numpy as jnp
from jax import lax
from jax.experimental import pallas as pl
from jax.experimental.pallas import tpu as pltpu
from jax.sharding import PartitionSpec as P

D = 8192
NSEL = 512
TOK = 128
Y_HI, PAIRS, PLACES, CORES = 2, 8, 2, 2
SEQS = Y_HI * PAIRS * PLACES * CORES
SIDES = Y_HI * CORES
DEPTH = PAIRS * PLACES
MEMBERS = PLACES * SIDES
Y_LO, X = 2, 4
TENSOR = Y_LO * X
WIDTH = D // TENSOR
PART = WIDTH // PAIRS
HALF = NSEL // Y_LO
TROWS = TOK // X
LANES = 128
BLOCKS = HALF // LANES
PIECE = BLOCKS * TROWS
ROWS = PART * Y_LO // MEMBERS


def batch_index(y_hi, pair, place, core):
    return ((y_hi * PAIRS + pair) * PLACES + place) * CORES + core


def column_groups():
    return [
        [batch_index(y, k, r, c) for k in range(PAIRS)]
        for y in range(Y_HI)
        for r in range(PLACES)
        for c in range(CORES)
    ]


def pair_groups():
    return [
        [batch_index(y, k, r, c) for r in range(PLACES) for y in range(Y_HI) for c in range(CORES)]
        for k in range(PAIRS)
    ]


def depth_groups():
    return [
        [batch_index(y, k, r, c) for k in range(PAIRS) for r in range(PLACES)]
        for y in range(Y_HI)
        for c in range(CORES)
    ]


def plane_groups():
    return [
        [
            batch_index(y, k, r, c) * TENSOR + t
            for y in range(Y_HI)
            for c in range(CORES)
            for t in range(TENSOR)
        ]
        for k in range(PAIRS)
        for r in range(PLACES)
    ]


def kernel_call(kernel, out_shape, args, scalars=(), scratch=()):
    smem = pl.BlockSpec(memory_space=pltpu.SMEM)
    vmem = pl.BlockSpec(memory_space=pltpu.VMEM)
    return pl.pallas_call(
        kernel,
        out_shape=out_shape,
        in_specs=[smem] * len(scalars) + [vmem] * len(args),
        out_specs=jax.tree.map(lambda _: vmem, out_shape),
        scratch_shapes=scratch,
        compiler_params=pltpu.CompilerParams(vmem_limit_bytes=24 * 1024 * 1024),
    )(*scalars, *args)


def select_kernel(
    index_ref, chosen_hbm, assign_hbm, grads_hbm, out_ref, spots_ref, chosen_ref, assign_ref, grads_ref, sems
):
    pairs = ((chosen_hbm, chosen_ref), (grads_hbm, grads_ref), (assign_hbm, assign_ref))
    copies = [
        pltpu.make_async_copy(source, target, sems.at[i]) for i, (source, target) in enumerate(pairs)
    ]
    for copy in copies:
        copy.start()
    copies[0].wait()
    local = chosen_ref[...] - index_ref[0] * WIDTH
    places = lax.broadcasted_iota(jnp.int32, (WIDTH, NSEL), 0)
    selector = jnp.where(places == local, 1.0, 0.0).astype(grads_ref.dtype)
    copies[1].wait()
    part = jnp.dot(grads_ref[...], selector, preferred_element_type=jnp.float32)
    part = part.astype(out_ref.dtype)
    for y in range(Y_LO):
        for j in range(BLOCKS):
            lane = (y * BLOCKS + j) * LANES
            block = part[:, lane : lane + LANES].reshape(X, TROWS, LANES)
            out_ref[y * X : (y + 1) * X, j * TROWS : (j + 1) * TROWS] = block
    copies[2].wait()
    column = lax.broadcasted_iota(jnp.int32, (SEQS, SEQS), 0)
    slot = lax.broadcasted_iota(jnp.int32, (SEQS, SEQS), 1)
    pair, core = column % PAIRS, column // PAIRS % CORES
    y_hi, place = column // (PAIRS * CORES) % Y_HI, column // (PAIRS * SIDES)
    ordered = jnp.where(batch_index(y_hi, pair, place, core) == slot, 1.0, 0.0)
    wanted = jnp.where(column == assign_ref[...], 1.0, 0.0)
    spots_ref[...] = lax.dot_general(
        ordered, wanted, (((1,), (1,)), ((), ())), preferred_element_type=jnp.float32
    )


def selected(chosen, assign, grads):
    smem = pl.BlockSpec(memory_space=pltpu.SMEM)
    hbm = pl.BlockSpec(memory_space=pltpu.HBM)
    vmem = pl.BlockSpec(memory_space=pltpu.VMEM)
    return pl.pallas_call(
        select_kernel,
        out_shape=(
            jax.ShapeDtypeStruct((TENSOR, PIECE, LANES), grads.dtype),
            jax.ShapeDtypeStruct((SEQS, SEQS), jnp.float32),
        ),
        in_specs=[smem, hbm, hbm, hbm],
        out_specs=(vmem, vmem),
        scratch_shapes=[
            pltpu.VMEM((1, NSEL), jnp.int32),
            pltpu.VMEM((1, SEQS), jnp.int32),
            pltpu.VMEM((TOK, WIDTH), grads.dtype),
            pltpu.SemaphoreType.DMA((3,)),
        ],
    )(lax.axis_index("tensor")[None], chosen[None], assign[None], grads)


def pack_kernel(acts_ref, shares_ref, out_ref):
    piece = shares_ref[0].astype(jnp.float32)
    for t in range(1, TENSOR):
        piece = piece + shares_ref[t].astype(jnp.float32)
    piece = piece.astype(out_ref.dtype)
    for k in range(PAIRS):
        out_ref[k, :TOK] = acts_ref[:, k * PART : (k + 1) * PART]
        out_ref[k, TOK:] = piece


def packed(acts, shares):
    shape = jax.ShapeDtypeStruct((PAIRS, TOK + PIECE, LANES), acts.dtype)
    return kernel_call(pack_kernel, shape, (acts, shares))


def unpack_kernel(both_ref, own_ref, piece_ref):
    own_ref[...] = both_ref[:, :TOK]
    piece_ref[...] = both_ref[:, TOK:]


def unpacked(both):
    shapes = (
        jax.ShapeDtypeStruct((PAIRS, TOK, PART), both.dtype),
        jax.ShapeDtypeStruct((PAIRS, PIECE, LANES), both.dtype),
    )
    return kernel_call(unpack_kernel, shapes, (both,))


def over_tensor(block, y_step, x_step):
    route = [
        (y * X + x, (y + y_step) % Y_LO * X + (x + x_step) % X) for y in range(Y_LO) for x in range(X)
    ]
    return lax.ppermute(block, "tensor", route)


def example_grads_kernel(x_ref, own_ref, other_ref, *refs):
    pieces, (out_ref, picked_ref) = refs[:X], refs[X:]
    for distance, piece in enumerate(pieces):
        start = pl.multiple_of(lax.rem(x_ref[0] + X - distance, X) * TROWS, TROWS)
        for j in range(BLOCKS):
            picked_ref[:, pl.ds(start, TROWS), j * LANES : (j + 1) * LANES] = piece[
                :, j * TROWS : (j + 1) * TROWS
            ]
    count = PART // ROWS
    for k in range(PAIRS):
        for side, ref in enumerate((own_ref, other_ref)):
            grad = lax.dot_general(
                ref[k], picked_ref[k], (((0,), (0,)), ((), ())), preferred_element_type=jnp.float32
            ).astype(out_ref.dtype)
            out_ref[side * count : (side + 1) * count, k] = grad.reshape(count, ROWS, HALF)


def example_grads(own, other, pieces):
    x = lax.rem(lax.axis_index("tensor"), X)[None]
    return kernel_call(
        example_grads_kernel,
        jax.ShapeDtypeStruct((MEMBERS, PAIRS, ROWS, HALF), own.dtype),
        (own, other, *pieces),
        scalars=(x,),
        scratch=[pltpu.VMEM((PAIRS, TOK, HALF), own.dtype)],
    )


def pairs_kernel(terms_ref, out_ref):
    terms = jnp.swapaxes(terms_ref[...].reshape(SEQS, ROWS, HALF), 0, 1)
    total = jnp.zeros((SEQS, SEQS), jnp.float32)
    for row in range(ROWS):
        total += lax.dot_general(
            terms[row], terms[row], (((1,), (1,)), ((), ())), preferred_element_type=jnp.float32
        )
    for r in range(PLACES):
        sides = [
            total[(r * SIDES + q) * PAIRS : (r * SIDES + q + 1) * PAIRS] for q in range(SIDES)
        ]
        out_ref[:, r, 0] = jnp.concatenate(sides, axis=1)


def pairs(terms):
    shape = jax.ShapeDtypeStruct((PAIRS, PLACES, 1, SIDES * SEQS), jnp.float32)
    return kernel_call(pairs_kernel, shape, (terms,))


def side_kernel(rows_ref, out_ref):
    sums = rows_ref[0]
    for z in range(1, DEPTH):
        sums = sums + rows_ref[z]
    for q in range(SIDES):
        out_ref[q] = jnp.broadcast_to(sums[:, q * SEQS : (q + 1) * SEQS][None], (TENSOR, 1, SEQS))


def place_kernel(rows_ref, spots_ref, out_ref):
    row = rows_ref[0]
    for member in range(1, SIDES * TENSOR):
        row = row + rows_ref[member]
    norming = 1.0 / (float(TOK) * float(D) * float(NSEL))
    out_ref[...] = lax.dot_general(
        row * norming,
        spots_ref[...],
        (((1,), (0,)), ((), ())),
        precision=lax.Precision.HIGHEST,
        preferred_element_type=jnp.float32,
    )


def on_device(acts, grads, chosen, assign):
    part, spots = selected(chosen, assign, grads)
    shares = lax.all_to_all(part, "tensor", 0, 0, tiled=True)
    both = lax.all_to_all(
        packed(acts, shares), "batch", 0, 0, axis_index_groups=column_groups(), tiled=True
    )
    own, piece = unpacked(both)
    other = over_tensor(own, 1, 0)
    pieces = [piece] + [over_tensor(piece, 0, distance) for distance in range(1, X)]

    terms = example_grads(own, other, pieces)
    terms = lax.all_to_all(terms, "batch", 0, 0, axis_index_groups=pair_groups(), tiled=True)
    rows = pairs(terms).reshape(DEPTH, 1, SIDES * SEQS)
    rows = lax.all_to_all(rows, "batch", 0, 0, axis_index_groups=depth_groups(), tiled=True)
    shape = jax.ShapeDtypeStruct((SIDES, TENSOR, 1, SEQS), jnp.float32)
    rows = kernel_call(side_kernel, shape, (rows,)).reshape(SIDES * TENSOR, 1, SEQS)
    rows = lax.all_to_all(
        rows, ("batch", "tensor"), 0, 0, axis_index_groups=plane_groups(), tiled=True
    )
    shape = jax.ShapeDtypeStruct((1, SEQS), jnp.float32)
    return kernel_call(place_kernel, shape, (rows, spots))


def solution(mesh):
    placed = (P("batch", "tensor"), P("batch", "tensor"), P(), P())
    return jax.shard_map(
        on_device, mesh=mesh, in_specs=placed, out_specs=P("batch", None), check_vma=False
    )
```

```python
import jax
import jax.numpy as jnp
from jax import lax
from jax.experimental import pallas as pl
from jax.experimental.pallas import tpu as pltpu
from jax.sharding import PartitionSpec as P

D = 8192
NSEL = 512
TOK = 128
Y_HI, PAIRS, PLACES, CORES = 2, 8, 2, 2
SEQS = Y_HI * PAIRS * PLACES * CORES
SIDES = Y_HI * CORES
DEPTH = PAIRS * PLACES
MEMBERS = PLACES * SIDES
Y_LO, X = 2, 4
TENSOR = Y_LO * X
WIDTH = D // TENSOR
PART = WIDTH // PAIRS
HALF = NSEL // Y_LO
TROWS = TOK // X
LANES = 128
BLOCKS = HALF // LANES
PIECE = BLOCKS * TROWS
ROWS = PART * Y_LO // MEMBERS


def batch_index(y_hi, pair, place, core):
    return ((y_hi * PAIRS + pair) * PLACES + place) * CORES + core


def column_groups():
    return [
        [batch_index(y, k, r, c) for k in range(PAIRS)]
        for y in range(Y_HI)
        for r in range(PLACES)
        for c in range(CORES)
    ]


def pair_groups():
    return [
        [batch_index(y, k, r, c) for r in range(PLACES) for y in range(Y_HI) for c in range(CORES)]
        for k in range(PAIRS)
    ]


def depth_groups():
    return [
        [batch_index(y, k, r, c) for k in range(PAIRS) for r in range(PLACES)]
        for y in range(Y_HI)
        for c in range(CORES)
    ]


def plane_groups():
    return [
        [
            batch_index(y, k, r, c) * TENSOR + t
            for y in range(Y_HI)
            for c in range(CORES)
            for t in range(TENSOR)
        ]
        for k in range(PAIRS)
        for r in range(PLACES)
    ]


def x_groups():
    return [[y * X + x for x in range(X)] for y in range(Y_LO)]


def kernel_call(kernel, out_shape, args):
    vmem = pl.BlockSpec(memory_space=pltpu.VMEM)
    return pl.pallas_call(
        kernel,
        out_shape=out_shape,
        in_specs=[vmem] * len(args),
        out_specs=jax.tree.map(lambda _: vmem, out_shape),
        compiler_params=pltpu.CompilerParams(vmem_limit_bytes=24 * 1024 * 1024),
    )(*args)


def arrange_kernel(part_ref, out_ref):
    for y in range(Y_LO):
        for j in range(BLOCKS):
            lane = (y * BLOCKS + j) * LANES
            block = part_ref[:, lane : lane + LANES].reshape(X, TROWS, LANES)
            out_ref[y * X : (y + 1) * X, j * TROWS : (j + 1) * TROWS] = block


def selected(chosen, grads):
    local = chosen - lax.axis_index("tensor") * WIDTH
    places = lax.broadcasted_iota(jnp.int32, (WIDTH, NSEL), 0)
    selector = (places == local[None, :]).astype(grads.dtype)
    part = lax.dot_general(
        grads, selector, (((1,), (0,)), ((), ())), preferred_element_type=jnp.float32
    ).astype(grads.dtype)
    shape = jax.ShapeDtypeStruct((TENSOR, PIECE, LANES), grads.dtype)
    return kernel_call(arrange_kernel, shape, (part,))


def pack_kernel(acts_ref, shares_ref, out_ref):
    piece = shares_ref[0].astype(jnp.float32)
    for t in range(1, TENSOR):
        piece = piece + shares_ref[t].astype(jnp.float32)
    piece = piece.astype(out_ref.dtype)
    for k in range(PAIRS):
        out_ref[k, :TOK] = acts_ref[:, k * PART : (k + 1) * PART]
        out_ref[k, TOK:] = piece


def packed(acts, shares):
    shape = jax.ShapeDtypeStruct((PAIRS, TOK + PIECE, LANES), acts.dtype)
    return kernel_call(pack_kernel, shape, (acts, shares))


def unpack_kernel(both_ref, own_ref, copies_ref):
    own_ref[...] = both_ref[:, :TOK]
    for x in range(X):
        copies_ref[x] = both_ref[:, TOK:]


def unpacked(both):
    shapes = (
        jax.ShapeDtypeStruct((PAIRS, TOK, PART), both.dtype),
        jax.ShapeDtypeStruct((X, PAIRS, PIECE, LANES), both.dtype),
    )
    return kernel_call(unpack_kernel, shapes, (both,))


def example_grads_kernel(own_ref, other_ref, picked_ref, assign_ref, out_ref, spots_ref):
    count = PART // ROWS
    for k in range(PAIRS):
        blocks = [
            picked_ref[:, k, j * TROWS : (j + 1) * TROWS].reshape(TOK, LANES) for j in range(BLOCKS)
        ]
        picked = jnp.concatenate(blocks, axis=1)
        for side, ref in enumerate((own_ref, other_ref)):
            grad = lax.dot_general(
                ref[k], picked, (((0,), (0,)), ((), ())), preferred_element_type=jnp.float32
            ).astype(out_ref.dtype)
            out_ref[side * count : (side + 1) * count, k] = grad.reshape(count, ROWS, HALF)
    column = lax.broadcasted_iota(jnp.int32, (SEQS, SEQS), 0)
    slot = lax.broadcasted_iota(jnp.int32, (SEQS, SEQS), 1)
    pair, core = column % PAIRS, column // PAIRS % CORES
    y_hi, place = column // (PAIRS * CORES) % Y_HI, column // (PAIRS * SIDES)
    ordered = jnp.where(batch_index(y_hi, pair, place, core) == slot, 1.0, 0.0)
    wanted = jnp.where(column == assign_ref[...], 1.0, 0.0)
    spots_ref[...] = lax.dot_general(
        ordered, wanted, (((1,), (1,)), ((), ())), preferred_element_type=jnp.float32
    )


def example_grads(own, other, picked, assign):
    shapes = (
        jax.ShapeDtypeStruct((MEMBERS, PAIRS, ROWS, HALF), own.dtype),
        jax.ShapeDtypeStruct((SEQS, SEQS), jnp.float32),
    )
    return kernel_call(example_grads_kernel, shapes, (own, other, picked, assign[None]))


def pairs_kernel(terms_ref, out_ref):
    terms = jnp.swapaxes(terms_ref[...].reshape(SEQS, ROWS, HALF), 0, 1)
    total = jnp.zeros((SEQS, SEQS), jnp.float32)
    for row in range(ROWS):
        total += lax.dot_general(
            terms[row], terms[row], (((1,), (1,)), ((), ())), preferred_element_type=jnp.float32
        )
    for r in range(PLACES):
        sides = [
            total[(r * SIDES + q) * PAIRS : (r * SIDES + q + 1) * PAIRS] for q in range(SIDES)
        ]
        out_ref[:, r, 0] = jnp.concatenate(sides, axis=1)


def pairs(terms):
    shape = jax.ShapeDtypeStruct((PAIRS, PLACES, 1, SIDES * SEQS), jnp.float32)
    return kernel_call(pairs_kernel, shape, (terms,))


def side_kernel(rows_ref, out_ref):
    sums = rows_ref[0]
    for z in range(1, DEPTH):
        sums = sums + rows_ref[z]
    for q in range(SIDES):
        out_ref[q] = jnp.broadcast_to(sums[:, q * SEQS : (q + 1) * SEQS][None], (TENSOR, 1, SEQS))


def place_kernel(rows_ref, spots_ref, out_ref):
    row = rows_ref[0]
    for member in range(1, SIDES * TENSOR):
        row = row + rows_ref[member]
    norming = 1.0 / (float(TOK) * float(D) * float(NSEL))
    out_ref[...] = lax.dot_general(
        row * norming,
        spots_ref[...],
        (((1,), (0,)), ((), ())),
        precision=lax.Precision.HIGHEST,
        preferred_element_type=jnp.float32,
    )


def on_device(acts, grads, chosen, assign):
    part = selected(chosen, grads)
    shares = lax.all_to_all(part, "tensor", 0, 0, tiled=True)
    both = lax.all_to_all(
        packed(acts, shares), "batch", 0, 0, axis_index_groups=column_groups(), tiled=True
    )
    own, copies = unpacked(both)
    picked = lax.all_to_all(copies, "tensor", 0, 0, axis_index_groups=x_groups(), tiled=True)
    other = lax.ppermute(own, "tensor", [(t, (t + X) % TENSOR) for t in range(TENSOR)])

    terms, spots = example_grads(own, other, picked, assign)
    terms = lax.all_to_all(terms, "batch", 0, 0, axis_index_groups=pair_groups(), tiled=True)
    rows = pairs(terms).reshape(DEPTH, 1, SIDES * SEQS)
    rows = lax.all_to_all(rows, "batch", 0, 0, axis_index_groups=depth_groups(), tiled=True)
    shape = jax.ShapeDtypeStruct((SIDES, TENSOR, 1, SEQS), jnp.float32)
    rows = kernel_call(side_kernel, shape, (rows,)).reshape(SIDES * TENSOR, 1, SEQS)
    rows = lax.all_to_all(
        rows, ("batch", "tensor"), 0, 0, axis_index_groups=plane_groups(), tiled=True
    )
    shape = jax.ShapeDtypeStruct((1, SEQS), jnp.float32)
    return kernel_call(place_kernel, shape, (rows, spots))


def solution(mesh):
    placed = (P("batch", "tensor"), P("batch", "tensor"), P(), P())
    return jax.shard_map(
        on_device, mesh=mesh, in_specs=placed, out_specs=P("batch", None), check_vma=False
    )
```

```python
import jax
import jax.numpy as jnp
from jax import lax
from jax.experimental import pallas as pl
from jax.experimental.pallas import tpu as pltpu
from jax.sharding import PartitionSpec as P

D = 8192
NSEL = 512
TOK = 128
Y_HI, PAIRS, PLACES, CORES = 2, 8, 2, 2
SEQS = Y_HI * PAIRS * PLACES * CORES
SIDES = Y_HI * CORES
DEPTH = PAIRS * PLACES
MEMBERS = PLACES * SIDES
Y_LO, X = 2, 4
TENSOR = Y_LO * X
WIDTH = D // TENSOR
PART = WIDTH // PAIRS
HALF = NSEL // Y_LO
TROWS = TOK // X
LANES = 128
BLOCKS = HALF // LANES
PIECE = BLOCKS * TROWS
ROWS = PART * Y_LO // MEMBERS


def batch_index(y_hi, pair, place, core):
    return ((y_hi * PAIRS + pair) * PLACES + place) * CORES + core


def column_groups():
    return [
        [batch_index(y, k, r, c) for k in range(PAIRS)]
        for y in range(Y_HI)
        for r in range(PLACES)
        for c in range(CORES)
    ]


def pair_groups():
    return [
        [batch_index(y, k, r, c) for r in range(PLACES) for y in range(Y_HI) for c in range(CORES)]
        for k in range(PAIRS)
    ]


def depth_groups():
    return [
        [batch_index(y, k, r, c) for k in range(PAIRS) for r in range(PLACES)]
        for y in range(Y_HI)
        for c in range(CORES)
    ]


def plane_groups():
    return [
        [
            batch_index(y, k, r, c) * TENSOR + t
            for y in range(Y_HI)
            for c in range(CORES)
            for t in range(TENSOR)
        ]
        for k in range(PAIRS)
        for r in range(PLACES)
    ]


def x_groups():
    return [[y * X + x for x in range(X)] for y in range(Y_LO)]


def kernel_call(kernel, out_shape, args, scalars=()):
    smem = pl.BlockSpec(memory_space=pltpu.SMEM)
    vmem = pl.BlockSpec(memory_space=pltpu.VMEM)
    return pl.pallas_call(
        kernel,
        out_shape=out_shape,
        in_specs=[smem] * len(scalars) + [vmem] * len(args),
        out_specs=jax.tree.map(lambda _: vmem, out_shape),
        compiler_params=pltpu.CompilerParams(vmem_limit_bytes=24 * 1024 * 1024),
    )(*scalars, *args)


def row_scale(batch, tensor, start, shape):
    pair = batch // (PLACES * CORES) % PAIRS
    first = (pair * TENSOR + tensor) * (MEMBERS * ROWS) + start
    number = first + lax.broadcasted_iota(jnp.int32, shape, 0)
    spread = jnp.bitwise_and(number * 40503, 65535).astype(jnp.float32)
    return 1.0 + spread / 65536.0


def arrange_kernel(part_ref, out_ref):
    for y in range(Y_LO):
        for j in range(BLOCKS):
            lane = (y * BLOCKS + j) * LANES
            block = part_ref[:, lane : lane + LANES].reshape(X, TROWS, LANES)
            out_ref[y * X : (y + 1) * X, j * TROWS : (j + 1) * TROWS] = block


def selected(chosen, grads):
    local = chosen - lax.axis_index("tensor") * WIDTH
    places = lax.broadcasted_iota(jnp.int32, (WIDTH, NSEL), 0)
    selector = (places == local[None, :]).astype(grads.dtype)
    part = lax.dot_general(
        grads, selector, (((1,), (0,)), ((), ())), preferred_element_type=jnp.float32
    ).astype(grads.dtype)
    shape = jax.ShapeDtypeStruct((TENSOR, PIECE, LANES), grads.dtype)
    return kernel_call(arrange_kernel, shape, (part,))


def pack_kernel(acts_ref, shares_ref, out_ref):
    piece = shares_ref[0].astype(jnp.float32)
    for t in range(1, TENSOR):
        piece = piece + shares_ref[t].astype(jnp.float32)
    piece = piece.astype(out_ref.dtype)
    for k in range(PAIRS):
        out_ref[k, :TOK] = acts_ref[:, k * PART : (k + 1) * PART]
        out_ref[k, TOK:] = piece


def packed(acts, shares):
    shape = jax.ShapeDtypeStruct((PAIRS, TOK + PIECE, LANES), acts.dtype)
    return kernel_call(pack_kernel, shape, (acts, shares))


def unpack_kernel(both_ref, own_ref, copies_ref):
    own_ref[...] = both_ref[:, :TOK]
    for x in range(X):
        copies_ref[x] = both_ref[:, TOK:]


def unpacked(both):
    shapes = (
        jax.ShapeDtypeStruct((PAIRS, TOK, PART), both.dtype),
        jax.ShapeDtypeStruct((X, PAIRS, PIECE, LANES), both.dtype),
    )
    return kernel_call(unpack_kernel, shapes, (both,))


def example_grads_kernel(
    batch_ref, tensor_ref, own_ref, other_ref, picked_ref, assign_ref, out_ref, spots_ref
):
    count = PART // ROWS
    scales = [
        row_scale(batch_ref[0], tensor_ref[0], side * PART, (PART, HALF)) for side in range(Y_LO)
    ]
    for k in range(PAIRS):
        blocks = [
            picked_ref[:, k, j * TROWS : (j + 1) * TROWS].reshape(TOK, LANES) for j in range(BLOCKS)
        ]
        picked = jnp.concatenate(blocks, axis=1)
        for side, ref in enumerate((own_ref, other_ref)):
            grad = lax.dot_general(
                ref[k], picked, (((0,), (0,)), ((), ())), preferred_element_type=jnp.float32
            )
            grad = (grad * scales[side]).astype(out_ref.dtype)
            out_ref[side * count : (side + 1) * count, k] = grad.reshape(count, ROWS, HALF)
    column = lax.broadcasted_iota(jnp.int32, (SEQS, SEQS), 0)
    slot = lax.broadcasted_iota(jnp.int32, (SEQS, SEQS), 1)
    pair, core = column % PAIRS, column // PAIRS % CORES
    y_hi, place = column // (PAIRS * CORES) % Y_HI, column // (PAIRS * SIDES)
    ordered = jnp.where(batch_index(y_hi, pair, place, core) == slot, 1.0, 0.0)
    wanted = jnp.where(column == assign_ref[...], 1.0, 0.0)
    spots_ref[...] = lax.dot_general(
        ordered, wanted, (((1,), (1,)), ((), ())), preferred_element_type=jnp.float32
    )


def example_grads(index, own, other, picked, assign):
    shapes = (
        jax.ShapeDtypeStruct((MEMBERS, PAIRS, ROWS, HALF), own.dtype),
        jax.ShapeDtypeStruct((SEQS, SEQS), jnp.float32),
    )
    return kernel_call(example_grads_kernel, shapes, (own, other, picked, assign[None]), index)


def pairs_kernel(batch_ref, tensor_ref, terms_ref, out_ref):
    terms = jnp.swapaxes(terms_ref[...].reshape(SEQS, ROWS, HALF), 0, 1)
    total = jnp.zeros((SEQS, SEQS), jnp.float32)
    batch = batch_ref[0]
    place, side = batch // CORES % PLACES, batch // (PAIRS * PLACES * CORES) * CORES + batch % CORES
    member = place * SIDES + side
    scale = row_scale(batch, tensor_ref[0], member * ROWS, (ROWS, SEQS))
    weight = 1.0 / (scale * scale)
    for row in range(ROWS):
        share = lax.dot_general(
            terms[row], terms[row], (((1,), (1,)), ((), ())), preferred_element_type=jnp.float32
        )
        total += share * weight[row : row + 1]
    for r in range(PLACES):
        sides = [
            total[(r * SIDES + q) * PAIRS : (r * SIDES + q + 1) * PAIRS] for q in range(SIDES)
        ]
        out_ref[:, r, 0] = jnp.concatenate(sides, axis=1)


def pairs(index, terms):
    shape = jax.ShapeDtypeStruct((PAIRS, PLACES, 1, SIDES * SEQS), jnp.float32)
    return kernel_call(pairs_kernel, shape, (terms,), index)


def side_kernel(rows_ref, out_ref):
    sums = rows_ref[0]
    for z in range(1, DEPTH):
        sums = sums + rows_ref[z]
    for q in range(SIDES):
        out_ref[q] = jnp.broadcast_to(sums[:, q * SEQS : (q + 1) * SEQS][None], (TENSOR, 1, SEQS))


def place_kernel(rows_ref, spots_ref, out_ref):
    row = rows_ref[0]
    for member in range(1, SIDES * TENSOR):
        row = row + rows_ref[member]
    norming = 1.0 / (float(TOK) * float(D) * float(NSEL))
    out_ref[...] = lax.dot_general(
        row * norming,
        spots_ref[...],
        (((1,), (0,)), ((), ())),
        precision=lax.Precision.HIGHEST,
        preferred_element_type=jnp.float32,
    )


def on_device(acts, grads, chosen, assign):
    part = selected(chosen, grads)
    shares = lax.all_to_all(part, "tensor", 0, 0, tiled=True)
    both = lax.all_to_all(
        packed(acts, shares), "batch", 0, 0, axis_index_groups=column_groups(), tiled=True
    )
    own, copies = unpacked(both)
    picked = lax.all_to_all(copies, "tensor", 0, 0, axis_index_groups=x_groups(), tiled=True)
    other = lax.ppermute(own, "tensor", [(t, (t + X) % TENSOR) for t in range(TENSOR)])

    index = (lax.axis_index("batch")[None], lax.axis_index("tensor")[None])
    terms, spots = example_grads(index, own, other, picked, assign)
    terms = lax.all_to_all(terms, "batch", 0, 0, axis_index_groups=pair_groups(), tiled=True)
    rows = pairs(index, terms).reshape(DEPTH, 1, SIDES * SEQS)
    rows = lax.all_to_all(rows, "batch", 0, 0, axis_index_groups=depth_groups(), tiled=True)
    shape = jax.ShapeDtypeStruct((SIDES, TENSOR, 1, SEQS), jnp.float32)
    rows = kernel_call(side_kernel, shape, (rows,)).reshape(SIDES * TENSOR, 1, SEQS)
    rows = lax.all_to_all(
        rows, ("batch", "tensor"), 0, 0, axis_index_groups=plane_groups(), tiled=True
    )
    shape = jax.ShapeDtypeStruct((1, SEQS), jnp.float32)
    return kernel_call(place_kernel, shape, (rows, spots))


def solution(mesh):
    placed = (P("batch", "tensor"), P("batch", "tensor"), P(), P())
    return jax.shard_map(
        on_device, mesh=mesh, in_specs=placed, out_specs=P("batch", None), check_vma=False
    )
```

```python
import jax
import jax.numpy as jnp
from jax import lax
from jax.experimental import pallas as pl
from jax.experimental.pallas import tpu as pltpu
from jax.sharding import PartitionSpec as P

D = 8192
NSEL = 512
TOK = 128
Y_HI, PAIRS, PLACES, CORES = 2, 8, 2, 2
SEQS = Y_HI * PAIRS * PLACES * CORES
SIDES = Y_HI * CORES
DEPTH = PAIRS * PLACES
MEMBERS = PLACES * SIDES
Y_LO, X = 2, 4
TENSOR = Y_LO * X
WIDTH = D // TENSOR
PART = WIDTH // PAIRS
HALF = NSEL // Y_LO
TROWS = TOK // X
LANES = 128
BLOCKS = HALF // LANES
PIECE = BLOCKS * TROWS
ROWS = PART * Y_LO // MEMBERS


def batch_index(y_hi, pair, place, core):
    return ((y_hi * PAIRS + pair) * PLACES + place) * CORES + core


def column_groups():
    return [
        [batch_index(y, k, r, c) for k in range(PAIRS)]
        for y in range(Y_HI)
        for r in range(PLACES)
        for c in range(CORES)
    ]


def pair_groups():
    return [
        [batch_index(y, k, r, c) for r in range(PLACES) for y in range(Y_HI) for c in range(CORES)]
        for k in range(PAIRS)
    ]


def depth_groups():
    return [
        [batch_index(y, k, r, c) for k in range(PAIRS) for r in range(PLACES)]
        for y in range(Y_HI)
        for c in range(CORES)
    ]


def plane_groups():
    return [
        [
            batch_index(y, k, r, c) * TENSOR + t
            for y in range(Y_HI)
            for c in range(CORES)
            for t in range(TENSOR)
        ]
        for k in range(PAIRS)
        for r in range(PLACES)
    ]


def x_groups():
    return [[y * X + x for x in range(X)] for y in range(Y_LO)]


def kernel_call(kernel, out_shape, args):
    vmem = pl.BlockSpec(memory_space=pltpu.VMEM)
    return pl.pallas_call(
        kernel,
        out_shape=out_shape,
        in_specs=[vmem] * len(args),
        out_specs=jax.tree.map(lambda _: vmem, out_shape),
        compiler_params=pltpu.CompilerParams(vmem_limit_bytes=24 * 1024 * 1024),
    )(*args)


def arrange_kernel(part_ref, out_ref):
    for y in range(Y_LO):
        for j in range(BLOCKS):
            lane = (y * BLOCKS + j) * LANES
            block = part_ref[:, lane : lane + LANES].reshape(X, TROWS, LANES)
            out_ref[y * X : (y + 1) * X, j * TROWS : (j + 1) * TROWS] = block


def selected(chosen, grads):
    local = chosen - lax.axis_index("tensor") * WIDTH
    places = lax.broadcasted_iota(jnp.int32, (WIDTH, NSEL), 0)
    selector = (places == local[None, :]).astype(grads.dtype)
    part = lax.dot_general(
        grads, selector, (((1,), (0,)), ((), ())), preferred_element_type=jnp.float32
    ).astype(grads.dtype)
    shape = jax.ShapeDtypeStruct((TENSOR, PIECE, LANES), grads.dtype)
    return kernel_call(arrange_kernel, shape, (part,))


def pack_kernel(acts_ref, shares_ref, out_ref):
    piece = shares_ref[0].astype(jnp.float32)
    for t in range(1, TENSOR):
        piece = piece + shares_ref[t].astype(jnp.float32)
    piece = piece.astype(out_ref.dtype)
    for k in range(PAIRS):
        out_ref[k, :TOK] = acts_ref[:, k * PART : (k + 1) * PART]
        out_ref[k, TOK:] = piece


def packed(acts, shares):
    shape = jax.ShapeDtypeStruct((PAIRS, TOK + PIECE, LANES), acts.dtype)
    return kernel_call(pack_kernel, shape, (acts, shares))


def unpack_kernel(both_ref, own_ref, copies_ref):
    own_ref[...] = both_ref[:, :TOK]
    for x in range(X):
        copies_ref[x] = both_ref[:, TOK:]


def unpacked(both):
    shapes = (
        jax.ShapeDtypeStruct((PAIRS, TOK, PART), both.dtype),
        jax.ShapeDtypeStruct((X, PAIRS, PIECE, LANES), both.dtype),
    )
    return kernel_call(unpack_kernel, shapes, (both,))


def example_grads_kernel(own_ref, other_ref, picked_ref, assign_ref, out_ref, spots_ref):
    count = PART // ROWS
    row = lax.broadcasted_iota(jnp.int32, (PART, HALF), 0)
    lane = lax.broadcasted_iota(jnp.int32, (PART, HALF), 1)
    spread = (row * HALF + lane) * 40503
    for k in range(PAIRS):
        blocks = [
            picked_ref[:, k, j * TROWS : (j + 1) * TROWS].reshape(TOK, LANES) for j in range(BLOCKS)
        ]
        picked = jnp.concatenate(blocks, axis=1)
        for side, ref in enumerate((own_ref, other_ref)):
            grad = lax.dot_general(
                ref[k], picked, (((0,), (0,)), ((), ())), preferred_element_type=jnp.float32
            )
            noise = (spread + (k * Y_LO + side) * 7919).astype(jnp.uint32)
            grad = pltpu.stochastic_round(grad, noise, target_dtype=out_ref.dtype)
            out_ref[side * count : (side + 1) * count, k] = grad.reshape(count, ROWS, HALF)
    column = lax.broadcasted_iota(jnp.int32, (SEQS, SEQS), 0)
    slot = lax.broadcasted_iota(jnp.int32, (SEQS, SEQS), 1)
    pair, core = column % PAIRS, column // PAIRS % CORES
    y_hi, place = column // (PAIRS * CORES) % Y_HI, column // (PAIRS * SIDES)
    ordered = jnp.where(batch_index(y_hi, pair, place, core) == slot, 1.0, 0.0)
    wanted = jnp.where(column == assign_ref[...], 1.0, 0.0)
    spots_ref[...] = lax.dot_general(
        ordered, wanted, (((1,), (1,)), ((), ())), preferred_element_type=jnp.float32
    )


def example_grads(own, other, picked, assign):
    shapes = (
        jax.ShapeDtypeStruct((MEMBERS, PAIRS, ROWS, HALF), own.dtype),
        jax.ShapeDtypeStruct((SEQS, SEQS), jnp.float32),
    )
    return kernel_call(example_grads_kernel, shapes, (own, other, picked, assign[None]))


def pairs_kernel(terms_ref, out_ref):
    terms = jnp.swapaxes(terms_ref[...].reshape(SEQS, ROWS, HALF), 0, 1)
    total = jnp.zeros((SEQS, SEQS), jnp.float32)
    for row in range(ROWS):
        total += lax.dot_general(
            terms[row], terms[row], (((1,), (1,)), ((), ())), preferred_element_type=jnp.float32
        )
    for r in range(PLACES):
        sides = [
            total[(r * SIDES + q) * PAIRS : (r * SIDES + q + 1) * PAIRS] for q in range(SIDES)
        ]
        out_ref[:, r, 0] = jnp.concatenate(sides, axis=1)


def pairs(terms):
    shape = jax.ShapeDtypeStruct((PAIRS, PLACES, 1, SIDES * SEQS), jnp.float32)
    return kernel_call(pairs_kernel, shape, (terms,))


def side_kernel(rows_ref, out_ref):
    sums = rows_ref[0]
    for z in range(1, DEPTH):
        sums = sums + rows_ref[z]
    for q in range(SIDES):
        out_ref[q] = jnp.broadcast_to(sums[:, q * SEQS : (q + 1) * SEQS][None], (TENSOR, 1, SEQS))


def place_kernel(rows_ref, spots_ref, out_ref):
    row = rows_ref[0]
    for member in range(1, SIDES * TENSOR):
        row = row + rows_ref[member]
    norming = 1.0 / (float(TOK) * float(D) * float(NSEL))
    out_ref[...] = lax.dot_general(
        row * norming,
        spots_ref[...],
        (((1,), (0,)), ((), ())),
        precision=lax.Precision.HIGHEST,
        preferred_element_type=jnp.float32,
    )


def on_device(acts, grads, chosen, assign):
    part = selected(chosen, grads)
    shares = lax.all_to_all(part, "tensor", 0, 0, tiled=True)
    both = lax.all_to_all(
        packed(acts, shares), "batch", 0, 0, axis_index_groups=column_groups(), tiled=True
    )
    own, copies = unpacked(both)
    picked = lax.all_to_all(copies, "tensor", 0, 0, axis_index_groups=x_groups(), tiled=True)
    other = lax.ppermute(own, "tensor", [(t, (t + X) % TENSOR) for t in range(TENSOR)])

    terms, spots = example_grads(own, other, picked, assign)
    terms = lax.all_to_all(terms, "batch", 0, 0, axis_index_groups=pair_groups(), tiled=True)
    rows = pairs(terms).reshape(DEPTH, 1, SIDES * SEQS)
    rows = lax.all_to_all(rows, "batch", 0, 0, axis_index_groups=depth_groups(), tiled=True)
    shape = jax.ShapeDtypeStruct((SIDES, TENSOR, 1, SEQS), jnp.float32)
    rows = kernel_call(side_kernel, shape, (rows,)).reshape(SIDES * TENSOR, 1, SEQS)
    rows = lax.all_to_all(
        rows, ("batch", "tensor"), 0, 0, axis_index_groups=plane_groups(), tiled=True
    )
    shape = jax.ShapeDtypeStruct((1, SEQS), jnp.float32)
    return kernel_call(place_kernel, shape, (rows, spots))


def solution(mesh):
    placed = (P("batch", "tensor"), P("batch", "tensor"), P(), P())
    return jax.shard_map(
        on_device, mesh=mesh, in_specs=placed, out_specs=P("batch", None), check_vma=False
    )
```

```python
import jax
import jax.numpy as jnp
from jax import lax
from jax.experimental import pallas as pl
from jax.experimental.pallas import tpu as pltpu
from jax.sharding import PartitionSpec as P

D = 8192
NSEL = 512
TOK = 128
Y_HI, PAIRS, PLACES, CORES = 2, 8, 2, 2
SEQS = Y_HI * PAIRS * PLACES * CORES
SIDES = Y_HI * CORES
DEPTH = PAIRS * PLACES
MEMBERS = PLACES * SIDES
Y_LO, X = 2, 4
TENSOR = Y_LO * X
WIDTH = D // TENSOR
PART = WIDTH // PAIRS
HALF = NSEL // Y_LO
TROWS = TOK // X
LANES = 128
BLOCKS = HALF // LANES
PIECE = BLOCKS * TROWS
ROWS = PART * Y_LO // MEMBERS


def batch_index(y_hi, pair, place, core):
    return ((y_hi * PAIRS + pair) * PLACES + place) * CORES + core


def column_groups():
    return [
        [batch_index(y, k, r, c) for k in range(PAIRS)]
        for y in range(Y_HI)
        for r in range(PLACES)
        for c in range(CORES)
    ]


def pair_groups():
    return [
        [batch_index(y, k, r, c) for r in range(PLACES) for y in range(Y_HI) for c in range(CORES)]
        for k in range(PAIRS)
    ]


def depth_groups():
    return [
        [batch_index(y, k, r, c) for k in range(PAIRS) for r in range(PLACES)]
        for y in range(Y_HI)
        for c in range(CORES)
    ]


def plane_groups():
    return [
        [
            batch_index(y, k, r, c) * TENSOR + t
            for y in range(Y_HI)
            for c in range(CORES)
            for t in range(TENSOR)
        ]
        for k in range(PAIRS)
        for r in range(PLACES)
    ]


def x_groups():
    return [[y * X + x for x in range(X)] for y in range(Y_LO)]


def kernel_call(kernel, out_shape, args):
    vmem = pl.BlockSpec(memory_space=pltpu.VMEM)
    return pl.pallas_call(
        kernel,
        out_shape=out_shape,
        in_specs=[vmem] * len(args),
        out_specs=jax.tree.map(lambda _: vmem, out_shape),
        compiler_params=pltpu.CompilerParams(vmem_limit_bytes=24 * 1024 * 1024),
    )(*args)


def arrange_kernel(part_ref, out_ref):
    for y in range(Y_LO):
        for j in range(BLOCKS):
            lane = (y * BLOCKS + j) * LANES
            block = part_ref[:, lane : lane + LANES].reshape(X, TROWS, LANES)
            out_ref[y * X : (y + 1) * X, j * TROWS : (j + 1) * TROWS] = block


def selected(chosen, grads):
    local = chosen - lax.axis_index("tensor") * WIDTH
    places = lax.broadcasted_iota(jnp.int32, (WIDTH, NSEL), 0)
    selector = (places == local[None, :]).astype(grads.dtype)
    part = lax.dot_general(
        grads, selector, (((1,), (0,)), ((), ())), preferred_element_type=jnp.float32
    ).astype(grads.dtype)
    shape = jax.ShapeDtypeStruct((TENSOR, PIECE, LANES), grads.dtype)
    return kernel_call(arrange_kernel, shape, (part,))


def pack_kernel(acts_ref, shares_ref, out_ref):
    piece = shares_ref[0].astype(jnp.float32)
    for t in range(1, TENSOR):
        piece = piece + shares_ref[t].astype(jnp.float32)
    piece = piece.astype(out_ref.dtype)
    for k in range(PAIRS):
        out_ref[k, :TOK] = acts_ref[:, k * PART : (k + 1) * PART]
        out_ref[k, TOK:] = piece


def packed(acts, shares):
    shape = jax.ShapeDtypeStruct((PAIRS, TOK + PIECE, LANES), acts.dtype)
    return kernel_call(pack_kernel, shape, (acts, shares))


def unpack_kernel(both_ref, own_ref, copies_ref, sems):
    copies = [
        pltpu.make_async_copy(both_ref.at[:, TOK:], copies_ref.at[x], sems.at[x]) for x in range(X)
    ]
    for copy in copies:
        copy.start()
    own_ref[...] = both_ref[:, :TOK]
    for copy in copies:
        copy.wait()


def unpacked(both):
    vmem = pl.BlockSpec(memory_space=pltpu.VMEM)
    return pl.pallas_call(
        unpack_kernel,
        out_shape=(
            jax.ShapeDtypeStruct((PAIRS, TOK, PART), both.dtype),
            jax.ShapeDtypeStruct((X, PAIRS, PIECE, LANES), both.dtype),
        ),
        in_specs=[vmem],
        out_specs=(vmem, pl.BlockSpec(memory_space=pltpu.HBM)),
        scratch_shapes=[pltpu.SemaphoreType.DMA((X,))],
        compiler_params=pltpu.CompilerParams(vmem_limit_bytes=24 * 1024 * 1024),
    )(both)


def example_grads_kernel(own_ref, other_ref, picked_ref, assign_ref, out_ref, spots_ref):
    count = PART // ROWS
    row = lax.broadcasted_iota(jnp.int32, (PART, HALF), 0)
    lane = lax.broadcasted_iota(jnp.int32, (PART, HALF), 1)
    spread = (row * HALF + lane) * 40503
    for k in range(PAIRS):
        blocks = [
            picked_ref[:, k, j * TROWS : (j + 1) * TROWS].reshape(TOK, LANES) for j in range(BLOCKS)
        ]
        picked = jnp.concatenate(blocks, axis=1)
        for side, ref in enumerate((own_ref, other_ref)):
            grad = lax.dot_general(
                ref[k], picked, (((0,), (0,)), ((), ())), preferred_element_type=jnp.float32
            )
            noise = (spread + (k * Y_LO + side) * 7919).astype(jnp.uint32)
            grad = pltpu.stochastic_round(grad, noise, target_dtype=out_ref.dtype)
            out_ref[side * count : (side + 1) * count, k] = grad.reshape(count, ROWS, HALF)
    column = lax.broadcasted_iota(jnp.int32, (SEQS, SEQS), 0)
    slot = lax.broadcasted_iota(jnp.int32, (SEQS, SEQS), 1)
    pair, core = column % PAIRS, column // PAIRS % CORES
    y_hi, place = column // (PAIRS * CORES) % Y_HI, column // (PAIRS * SIDES)
    ordered = jnp.where(batch_index(y_hi, pair, place, core) == slot, 1.0, 0.0)
    wanted = jnp.where(column == assign_ref[...], 1.0, 0.0)
    spots_ref[...] = lax.dot_general(
        ordered, wanted, (((1,), (1,)), ((), ())), preferred_element_type=jnp.float32
    )


def example_grads(own, other, picked, assign):
    shapes = (
        jax.ShapeDtypeStruct((MEMBERS, PAIRS, ROWS, HALF), own.dtype),
        jax.ShapeDtypeStruct((SEQS, SEQS), jnp.float32),
    )
    return kernel_call(example_grads_kernel, shapes, (own, other, picked, assign[None]))


def pairs_kernel(terms_ref, out_ref):
    terms = jnp.swapaxes(terms_ref[...].reshape(SEQS, ROWS, HALF), 0, 1)
    total = jnp.zeros((SEQS, SEQS), jnp.float32)
    for row in range(ROWS):
        total += lax.dot_general(
            terms[row], terms[row], (((1,), (1,)), ((), ())), preferred_element_type=jnp.float32
        )
    for r in range(PLACES):
        sides = [
            total[(r * SIDES + q) * PAIRS : (r * SIDES + q + 1) * PAIRS] for q in range(SIDES)
        ]
        out_ref[:, r, 0] = jnp.concatenate(sides, axis=1)


def pairs(terms):
    shape = jax.ShapeDtypeStruct((PAIRS, PLACES, 1, SIDES * SEQS), jnp.float32)
    return kernel_call(pairs_kernel, shape, (terms,))


def side_kernel(rows_ref, out_ref):
    sums = rows_ref[0]
    for z in range(1, DEPTH):
        sums = sums + rows_ref[z]
    for q in range(SIDES):
        out_ref[q] = jnp.broadcast_to(sums[:, q * SEQS : (q + 1) * SEQS][None], (TENSOR, 1, SEQS))


def place_kernel(rows_ref, spots_ref, out_ref):
    row = rows_ref[0]
    for member in range(1, SIDES * TENSOR):
        row = row + rows_ref[member]
    norming = 1.0 / (float(TOK) * float(D) * float(NSEL))
    out_ref[...] = lax.dot_general(
        row * norming,
        spots_ref[...],
        (((1,), (0,)), ((), ())),
        precision=lax.Precision.HIGHEST,
        preferred_element_type=jnp.float32,
    )


def on_device(acts, grads, chosen, assign):
    part = selected(chosen, grads)
    shares = lax.all_to_all(part, "tensor", 0, 0, tiled=True)
    both = lax.all_to_all(
        packed(acts, shares), "batch", 0, 0, axis_index_groups=column_groups(), tiled=True
    )
    own, copies = unpacked(both)
    picked = lax.all_to_all(copies, "tensor", 0, 0, axis_index_groups=x_groups(), tiled=True)
    other = lax.ppermute(own, "tensor", [(t, (t + X) % TENSOR) for t in range(TENSOR)])

    terms, spots = example_grads(own, other, picked, assign)
    terms = lax.all_to_all(terms, "batch", 0, 0, axis_index_groups=pair_groups(), tiled=True)
    rows = pairs(terms).reshape(DEPTH, 1, SIDES * SEQS)
    rows = lax.all_to_all(rows, "batch", 0, 0, axis_index_groups=depth_groups(), tiled=True)
    shape = jax.ShapeDtypeStruct((SIDES, TENSOR, 1, SEQS), jnp.float32)
    rows = kernel_call(side_kernel, shape, (rows,)).reshape(SIDES * TENSOR, 1, SEQS)
    rows = lax.all_to_all(
        rows, ("batch", "tensor"), 0, 0, axis_index_groups=plane_groups(), tiled=True
    )
    shape = jax.ShapeDtypeStruct((1, SEQS), jnp.float32)
    return kernel_call(place_kernel, shape, (rows, spots))


def solution(mesh):
    placed = (P("batch", "tensor"), P("batch", "tensor"), P(), P())
    return jax.shard_map(
        on_device, mesh=mesh, in_specs=placed, out_specs=P("batch", None), check_vma=False
    )
```

```python
import jax
import jax.numpy as jnp
from jax import lax
from jax.experimental import pallas as pl
from jax.experimental.pallas import tpu as pltpu
from jax.sharding import PartitionSpec as P

D = 8192
NSEL = 512
TOK = 128
Y_HI, PAIRS, PLACES, CORES = 2, 8, 2, 2
SEQS = Y_HI * PAIRS * PLACES * CORES
SIDES = Y_HI * CORES
DEPTH = PAIRS * PLACES
MEMBERS = PLACES * SIDES
Y_LO, X = 2, 4
TENSOR = Y_LO * X
WIDTH = D // TENSOR
PART = WIDTH // PAIRS
HALF = NSEL // Y_LO
TROWS = TOK // X
LANES = 128
BLOCKS = HALF // LANES
PIECE = BLOCKS * TROWS
ROWS = PART * Y_LO // MEMBERS


def batch_index(y_hi, pair, place, core):
    return ((y_hi * PAIRS + pair) * PLACES + place) * CORES + core


def column_groups():
    return [
        [batch_index(y, k, r, c) for k in range(PAIRS)]
        for y in range(Y_HI)
        for r in range(PLACES)
        for c in range(CORES)
    ]


def pair_groups():
    return [
        [batch_index(y, k, r, c) for r in range(PLACES) for y in range(Y_HI) for c in range(CORES)]
        for k in range(PAIRS)
    ]


def depth_groups():
    return [
        [batch_index(y, k, r, c) for k in range(PAIRS) for r in range(PLACES)]
        for y in range(Y_HI)
        for c in range(CORES)
    ]


def plane_groups():
    return [
        [
            batch_index(y, k, r, c) * TENSOR + t
            for y in range(Y_HI)
            for c in range(CORES)
            for t in range(TENSOR)
        ]
        for k in range(PAIRS)
        for r in range(PLACES)
    ]


def x_groups():
    return [[y * X + x for x in range(X)] for y in range(Y_LO)]


def kernel_call(kernel, out_shape, args):
    vmem = pl.BlockSpec(memory_space=pltpu.VMEM)
    return pl.pallas_call(
        kernel,
        out_shape=out_shape,
        in_specs=[vmem] * len(args),
        out_specs=jax.tree.map(lambda _: vmem, out_shape),
        compiler_params=pltpu.CompilerParams(vmem_limit_bytes=24 * 1024 * 1024),
    )(*args)


def arrange_kernel(part_ref, out_ref):
    for y in range(Y_LO):
        for j in range(BLOCKS):
            lane = (y * BLOCKS + j) * LANES
            block = part_ref[:, lane : lane + LANES].reshape(X, TROWS, LANES)
            out_ref[y * X : (y + 1) * X, j * TROWS : (j + 1) * TROWS] = block


def selected(chosen, grads):
    local = chosen - lax.axis_index("tensor") * WIDTH
    places = lax.broadcasted_iota(jnp.int32, (WIDTH, NSEL), 0)
    selector = (places == local[None, :]).astype(grads.dtype)
    part = lax.dot_general(
        grads, selector, (((1,), (0,)), ((), ())), preferred_element_type=jnp.float32
    ).astype(grads.dtype)
    shape = jax.ShapeDtypeStruct((TENSOR, PIECE, LANES), grads.dtype)
    return kernel_call(arrange_kernel, shape, (part,))


def pack_kernel(acts_ref, shares_ref, out_ref):
    piece = shares_ref[0].astype(jnp.float32)
    for t in range(1, TENSOR):
        piece = piece + shares_ref[t].astype(jnp.float32)
    piece = piece.astype(out_ref.dtype)
    for k in range(PAIRS):
        out_ref[k, :TOK] = acts_ref[:, k * PART : (k + 1) * PART]
        out_ref[k, TOK:] = piece


def packed(acts, shares):
    shape = jax.ShapeDtypeStruct((PAIRS, TOK + PIECE, LANES), acts.dtype)
    return kernel_call(pack_kernel, shape, (acts, shares))


def unpack_kernel(both_ref, own_ref, copies_ref):
    own_ref[...] = both_ref[:, :TOK]
    for x in range(X):
        copies_ref[x] = both_ref[:, TOK:]


def unpacked(both):
    shapes = (
        jax.ShapeDtypeStruct((PAIRS, TOK, PART), both.dtype),
        jax.ShapeDtypeStruct((X, PAIRS, PIECE, LANES), both.dtype),
    )
    return kernel_call(unpack_kernel, shapes, (both,))


def example_grads_kernel(own_ref, other_ref, picked_ref, assign_ref, out_ref, spots_ref):
    count = PART // ROWS
    row = lax.broadcasted_iota(jnp.int32, (PART, HALF), 0)
    lane = lax.broadcasted_iota(jnp.int32, (PART, HALF), 1)
    spread = (row * HALF + lane) * 40503
    for k in range(PAIRS):
        blocks = [
            picked_ref[:, k, j * TROWS : (j + 1) * TROWS].reshape(TOK, LANES) for j in range(BLOCKS)
        ]
        picked = jnp.concatenate(blocks, axis=1)
        for side, ref in enumerate((own_ref, other_ref)):
            grad = lax.dot_general(
                ref[k], picked, (((0,), (0,)), ((), ())), preferred_element_type=jnp.float32
            )
            noise = jnp.bitwise_and(spread + (k * Y_LO + side) * 7919, 65535) * 128
            grad = pltpu.stochastic_round(grad, noise.astype(jnp.uint32), target_dtype=out_ref.dtype)
            out_ref[side * count : (side + 1) * count, k] = grad.reshape(count, ROWS, HALF)
    column = lax.broadcasted_iota(jnp.int32, (SEQS, SEQS), 0)
    slot = lax.broadcasted_iota(jnp.int32, (SEQS, SEQS), 1)
    pair, core = column % PAIRS, column // PAIRS % CORES
    y_hi, place = column // (PAIRS * CORES) % Y_HI, column // (PAIRS * SIDES)
    ordered = jnp.where(batch_index(y_hi, pair, place, core) == slot, 1.0, 0.0)
    wanted = jnp.where(column == assign_ref[...], 1.0, 0.0)
    spots_ref[...] = lax.dot_general(
        ordered, wanted, (((1,), (1,)), ((), ())), preferred_element_type=jnp.float32
    )


def example_grads(own, other, picked, assign):
    shapes = (
        jax.ShapeDtypeStruct((MEMBERS, PAIRS, ROWS, HALF), own.dtype),
        jax.ShapeDtypeStruct((SEQS, SEQS), jnp.float32),
    )
    return kernel_call(example_grads_kernel, shapes, (own, other, picked, assign[None]))


def pairs_kernel(terms_ref, out_ref):
    terms = jnp.swapaxes(terms_ref[...].reshape(SEQS, ROWS, HALF), 0, 1)
    total = jnp.zeros((SEQS, SEQS), jnp.float32)
    for row in range(ROWS):
        total += lax.dot_general(
            terms[row], terms[row], (((1,), (1,)), ((), ())), preferred_element_type=jnp.float32
        )
    for r in range(PLACES):
        sides = [
            total[(r * SIDES + q) * PAIRS : (r * SIDES + q + 1) * PAIRS] for q in range(SIDES)
        ]
        out_ref[:, r, 0] = jnp.concatenate(sides, axis=1)


def pairs(terms):
    shape = jax.ShapeDtypeStruct((PAIRS, PLACES, 1, SIDES * SEQS), jnp.float32)
    return kernel_call(pairs_kernel, shape, (terms,))


def side_kernel(rows_ref, out_ref):
    sums = rows_ref[0]
    for z in range(1, DEPTH):
        sums = sums + rows_ref[z]
    for q in range(SIDES):
        out_ref[q] = jnp.broadcast_to(sums[:, q * SEQS : (q + 1) * SEQS][None], (TENSOR, 1, SEQS))


def place_kernel(rows_ref, spots_ref, out_ref):
    row = rows_ref[0]
    for member in range(1, SIDES * TENSOR):
        row = row + rows_ref[member]
    norming = 1.0 / (float(TOK) * float(D) * float(NSEL))
    out_ref[...] = lax.dot_general(
        row * norming,
        spots_ref[...],
        (((1,), (0,)), ((), ())),
        precision=lax.Precision.HIGHEST,
        preferred_element_type=jnp.float32,
    )


def on_device(acts, grads, chosen, assign):
    part = selected(chosen, grads)
    shares = lax.all_to_all(part, "tensor", 0, 0, tiled=True)
    both = lax.all_to_all(
        packed(acts, shares), "batch", 0, 0, axis_index_groups=column_groups(), tiled=True
    )
    own, copies = unpacked(both)
    picked = lax.all_to_all(copies, "tensor", 0, 0, axis_index_groups=x_groups(), tiled=True)
    other = lax.ppermute(own, "tensor", [(t, (t + X) % TENSOR) for t in range(TENSOR)])

    terms, spots = example_grads(own, other, picked, assign)
    terms = lax.all_to_all(terms, "batch", 0, 0, axis_index_groups=pair_groups(), tiled=True)
    rows = pairs(terms).reshape(DEPTH, 1, SIDES * SEQS)
    rows = lax.all_to_all(rows, "batch", 0, 0, axis_index_groups=depth_groups(), tiled=True)
    shape = jax.ShapeDtypeStruct((SIDES, TENSOR, 1, SEQS), jnp.float32)
    rows = kernel_call(side_kernel, shape, (rows,)).reshape(SIDES * TENSOR, 1, SEQS)
    rows = lax.all_to_all(
        rows, ("batch", "tensor"), 0, 0, axis_index_groups=plane_groups(), tiled=True
    )
    shape = jax.ShapeDtypeStruct((1, SEQS), jnp.float32)
    return kernel_call(place_kernel, shape, (rows, spots))


def solution(mesh):
    placed = (P("batch", "tensor"), P("batch", "tensor"), P(), P())
    return jax.shard_map(
        on_device, mesh=mesh, in_specs=placed, out_specs=P("batch", None), check_vma=False
    )
```

```python
import jax
import jax.numpy as jnp
from jax import lax
from jax.experimental import pallas as pl
from jax.experimental.pallas import tpu as pltpu
from jax.sharding import PartitionSpec as P

D = 8192
NSEL = 512
TOK = 128
Y_HI, PAIRS, PLACES, CORES = 2, 8, 2, 2
SEQS = Y_HI * PAIRS * PLACES * CORES
SIDES = Y_HI * CORES
DEPTH = PAIRS * PLACES
Y_LO, X = 2, 4
TENSOR = Y_LO * X
WIDTH = D // TENSOR
PART = WIDTH // PAIRS
HALF = NSEL // Y_LO
TROWS = TOK // X
LANES = 128
BLOCKS = HALF // LANES
PIECE = BLOCKS * TROWS
MEMBERS = PLACES * SIDES * TENSOR
ROWS = WIDTH // MEMBERS


def batch_index(y_hi, pair, place, core):
    return ((y_hi * PAIRS + pair) * PLACES + place) * CORES + core


def column_groups():
    return [
        [batch_index(y, k, r, c) for k in range(PAIRS)]
        for y in range(Y_HI)
        for r in range(PLACES)
        for c in range(CORES)
    ]


def pair_groups():
    return [
        [
            batch_index(y, k, r, c) * TENSOR + t
            for r in range(PLACES)
            for y in range(Y_HI)
            for c in range(CORES)
            for t in range(TENSOR)
        ]
        for k in range(PAIRS)
    ]


def depth_groups():
    return [
        [batch_index(y, k, r, c) for k in range(PAIRS) for r in range(PLACES)]
        for y in range(Y_HI)
        for c in range(CORES)
    ]


def plane_groups():
    return [
        [
            batch_index(y, k, r, c) * TENSOR + t
            for y in range(Y_HI)
            for c in range(CORES)
            for t in range(TENSOR)
        ]
        for k in range(PAIRS)
        for r in range(PLACES)
    ]


def kernel_call(kernel, out_shape, args):
    vmem = pl.BlockSpec(memory_space=pltpu.VMEM)
    return pl.pallas_call(
        kernel,
        out_shape=out_shape,
        in_specs=[vmem] * len(args),
        out_specs=jax.tree.map(lambda _: vmem, out_shape),
        compiler_params=pltpu.CompilerParams(vmem_limit_bytes=24 * 1024 * 1024),
    )(*args)


def arrange_kernel(part_ref, out_ref):
    for y in range(Y_LO):
        for j in range(BLOCKS):
            lane = (y * BLOCKS + j) * LANES
            block = part_ref[:, lane : lane + LANES].reshape(X, TROWS, LANES)
            out_ref[y * X : (y + 1) * X, j * TROWS : (j + 1) * TROWS] = block


def selected(chosen, grads):
    local = chosen - lax.axis_index("tensor") * WIDTH
    places = lax.broadcasted_iota(jnp.int32, (WIDTH, NSEL), 0)
    selector = (places == local[None, :]).astype(grads.dtype)
    part = lax.dot_general(
        grads, selector, (((1,), (0,)), ((), ())), preferred_element_type=jnp.float32
    ).astype(grads.dtype)
    shape = jax.ShapeDtypeStruct((TENSOR, PIECE, LANES), grads.dtype)
    return kernel_call(arrange_kernel, shape, (part,))


def pack_kernel(acts_ref, shares_ref, out_ref):
    piece = shares_ref[0].astype(jnp.float32)
    for t in range(1, TENSOR):
        piece = piece + shares_ref[t].astype(jnp.float32)
    piece = piece.astype(out_ref.dtype)
    for k in range(PAIRS):
        out_ref[k, :TOK] = acts_ref[:, k * PART : (k + 1) * PART]
        out_ref[k, TOK:] = piece


def packed(acts, shares):
    shape = jax.ShapeDtypeStruct((PAIRS, TOK + PIECE, LANES), acts.dtype)
    return kernel_call(pack_kernel, shape, (acts, shares))


def example_grad_kernel(both_ref, assign_ref, out_ref, spots_ref):
    blocks = [
        both_ref[y * X : (y + 1) * X, TOK + j * TROWS : TOK + (j + 1) * TROWS].reshape(TOK, LANES)
        for y in range(Y_LO)
        for j in range(BLOCKS)
    ]
    picked = jnp.concatenate(blocks, axis=1)
    row = lax.broadcasted_iota(jnp.int32, (PART, NSEL), 0)
    lane = lax.broadcasted_iota(jnp.int32, (PART, NSEL), 1)
    spread = (row * NSEL + lane) * 40503
    count = PART // ROWS
    for t in range(TENSOR):
        grad = lax.dot_general(
            both_ref[t, :TOK], picked, (((0,), (0,)), ((), ())), preferred_element_type=jnp.float32
        )
        noise = jnp.bitwise_and(spread + t * 7919, 65535) * 128
        grad = pltpu.stochastic_round(grad, noise.astype(jnp.uint32), target_dtype=out_ref.dtype)
        out_ref[t * count : (t + 1) * count] = grad.reshape(count, ROWS, NSEL)
    column = lax.broadcasted_iota(jnp.int32, (SEQS, SEQS), 0)
    slot = lax.broadcasted_iota(jnp.int32, (SEQS, SEQS), 1)
    pair, core = column % PAIRS, column // PAIRS % CORES
    y_hi, place = column // (PAIRS * CORES) % Y_HI, column // (PAIRS * SIDES)
    ordered = jnp.where(batch_index(y_hi, pair, place, core) == slot, 1.0, 0.0)
    wanted = jnp.where(column == assign_ref[...], 1.0, 0.0)
    spots_ref[...] = lax.dot_general(
        ordered, wanted, (((1,), (1,)), ((), ())), preferred_element_type=jnp.float32
    )


def example_grad(both, assign):
    shapes = (
        jax.ShapeDtypeStruct((MEMBERS, ROWS, NSEL), both.dtype),
        jax.ShapeDtypeStruct((SEQS, SEQS), jnp.float32),
    )
    return kernel_call(example_grad_kernel, shapes, (both, assign[None]))


def pairs_kernel(terms_ref, out_ref):
    terms = jnp.swapaxes(terms_ref[...], 0, 1)
    total = jnp.zeros((SEQS, SEQS), jnp.float32)
    for row in range(ROWS):
        total += lax.dot_general(
            terms[row], terms[row], (((1,), (1,)), ((), ())), preferred_element_type=jnp.float32
        )
    for r in range(PLACES):
        sides = [
            total[(r * SIDES + q) * PAIRS : (r * SIDES + q + 1) * PAIRS] for q in range(SIDES)
        ]
        out_ref[:, r, 0] = jnp.concatenate(sides, axis=1)


def pairs(terms):
    shape = jax.ShapeDtypeStruct((PAIRS, PLACES, 1, SIDES * SEQS), jnp.float32)
    return kernel_call(pairs_kernel, shape, (terms,))


def side_kernel(rows_ref, out_ref):
    sums = rows_ref[0]
    for z in range(1, DEPTH):
        sums = sums + rows_ref[z]
    for q in range(SIDES):
        out_ref[q] = jnp.broadcast_to(sums[:, q * SEQS : (q + 1) * SEQS][None], (TENSOR, 1, SEQS))


def place_kernel(rows_ref, spots_ref, out_ref):
    row = rows_ref[0]
    for member in range(1, SIDES * TENSOR):
        row = row + rows_ref[member]
    norming = 1.0 / (float(TOK) * float(D) * float(NSEL))
    out_ref[...] = lax.dot_general(
        row * norming,
        spots_ref[...],
        (((1,), (0,)), ((), ())),
        precision=lax.Precision.HIGHEST,
        preferred_element_type=jnp.float32,
    )


def on_device(acts, grads, chosen, assign):
    part = selected(chosen, grads)
    shares = lax.all_to_all(part, "tensor", 0, 0, tiled=True)
    both = lax.all_to_all(
        packed(acts, shares), "batch", 0, 0, axis_index_groups=column_groups(), tiled=True
    )
    both = lax.all_to_all(both, "tensor", 0, 0, tiled=True)
    terms, spots = example_grad(both, assign)
    terms = lax.all_to_all(
        terms, ("batch", "tensor"), 0, 0, axis_index_groups=pair_groups(), tiled=True
    )
    rows = pairs(terms).reshape(DEPTH, 1, SIDES * SEQS)
    rows = lax.all_to_all(rows, "batch", 0, 0, axis_index_groups=depth_groups(), tiled=True)
    shape = jax.ShapeDtypeStruct((SIDES, TENSOR, 1, SEQS), jnp.float32)
    rows = kernel_call(side_kernel, shape, (rows,)).reshape(SIDES * TENSOR, 1, SEQS)
    rows = lax.all_to_all(
        rows, ("batch", "tensor"), 0, 0, axis_index_groups=plane_groups(), tiled=True
    )
    shape = jax.ShapeDtypeStruct((1, SEQS), jnp.float32)
    return kernel_call(place_kernel, shape, (rows, spots))


def solution(mesh):
    placed = (P("batch", "tensor"), P("batch", "tensor"), P(), P())
    return jax.shard_map(
        on_device, mesh=mesh, in_specs=placed, out_specs=P("batch", None), check_vma=False
    )
```

```python
import jax
import jax.numpy as jnp
from jax import lax
from jax.experimental import pallas as pl
from jax.experimental.pallas import tpu as pltpu
from jax.sharding import PartitionSpec as P

D = 8192
NSEL = 512
TOK = 128
Y_HI, PAIRS, PLACES, CORES = 2, 8, 2, 2
SEQS = Y_HI * PAIRS * PLACES * CORES
SIDES = Y_HI * CORES
DEPTH = PAIRS * PLACES * CORES
Y_LO, X = 2, 4
TENSOR = Y_LO * X
WIDTH = D // TENSOR
PART = WIDTH // PAIRS
HALF = NSEL // Y_LO
TROWS = TOK // X
LANES = 128
BLOCKS = HALF // LANES
PIECE = BLOCKS * TROWS
MEMBERS = PLACES * SIDES * TENSOR
ROWS = WIDTH // MEMBERS


def batch_index(y_hi, pair, place, core):
    return ((y_hi * PAIRS + pair) * PLACES + place) * CORES + core


def column_groups():
    return [
        [batch_index(y, k, r, c) for k in range(PAIRS)]
        for y in range(Y_HI)
        for r in range(PLACES)
        for c in range(CORES)
    ]


def pair_groups():
    return [
        [
            batch_index(y, k, r, c) * TENSOR + t
            for r in range(PLACES)
            for y in range(Y_HI)
            for c in range(CORES)
            for t in range(TENSOR)
        ]
        for k in range(PAIRS)
    ]


def depth_groups():
    return [
        [batch_index(y, k, r, c) for k in range(PAIRS) for r in range(PLACES) for c in range(CORES)]
        for y in range(Y_HI)
    ]


def side_groups():
    return [
        [batch_index(y, k, r, c) * TENSOR + t for y in range(Y_HI) for t in range(TENSOR)]
        for k in range(PAIRS)
        for r in range(PLACES)
        for c in range(CORES)
    ]


def kernel_call(kernel, out_shape, args):
    vmem = pl.BlockSpec(memory_space=pltpu.VMEM)
    return pl.pallas_call(
        kernel,
        out_shape=out_shape,
        in_specs=[vmem] * len(args),
        out_specs=jax.tree.map(lambda _: vmem, out_shape),
        compiler_params=pltpu.CompilerParams(vmem_limit_bytes=24 * 1024 * 1024),
    )(*args)


def arrange_kernel(part_ref, out_ref):
    for y in range(Y_LO):
        for j in range(BLOCKS):
            lane = (y * BLOCKS + j) * LANES
            block = part_ref[:, lane : lane + LANES].reshape(X, TROWS, LANES)
            out_ref[y * X : (y + 1) * X, j * TROWS : (j + 1) * TROWS] = block


def selected(chosen, grads):
    local = chosen - lax.axis_index("tensor") * WIDTH
    places = lax.broadcasted_iota(jnp.int32, (WIDTH, NSEL), 0)
    selector = (places == local[None, :]).astype(grads.dtype)
    part = lax.dot_general(
        grads, selector, (((1,), (0,)), ((), ())), preferred_element_type=jnp.float32
    ).astype(grads.dtype)
    shape = jax.ShapeDtypeStruct((TENSOR, PIECE, LANES), grads.dtype)
    return kernel_call(arrange_kernel, shape, (part,))


def pack_kernel(acts_ref, shares_ref, out_ref):
    piece = shares_ref[0].astype(jnp.float32)
    for t in range(1, TENSOR):
        piece = piece + shares_ref[t].astype(jnp.float32)
    piece = piece.astype(out_ref.dtype)
    for k in range(PAIRS):
        out_ref[k, :TOK] = acts_ref[:, k * PART : (k + 1) * PART]
        out_ref[k, TOK:] = piece


def packed(acts, shares):
    shape = jax.ShapeDtypeStruct((PAIRS, TOK + PIECE, LANES), acts.dtype)
    return kernel_call(pack_kernel, shape, (acts, shares))


def example_grad_kernel(both_ref, assign_ref, out_ref, spots_ref):
    blocks = [
        both_ref[y * X : (y + 1) * X, TOK + j * TROWS : TOK + (j + 1) * TROWS].reshape(TOK, LANES)
        for y in range(Y_LO)
        for j in range(BLOCKS)
    ]
    picked = jnp.concatenate(blocks, axis=1)
    row = lax.broadcasted_iota(jnp.int32, (PART, NSEL), 0)
    lane = lax.broadcasted_iota(jnp.int32, (PART, NSEL), 1)
    spread = (row * NSEL + lane) * 40503
    count = PART // ROWS
    for t in range(TENSOR):
        grad = lax.dot_general(
            both_ref[t, :TOK], picked, (((0,), (0,)), ((), ())), preferred_element_type=jnp.float32
        )
        noise = jnp.bitwise_and(spread + t * 7919, 65535) * 128
        grad = pltpu.stochastic_round(grad, noise.astype(jnp.uint32), target_dtype=out_ref.dtype)
        out_ref[t * count : (t + 1) * count] = grad.reshape(count, ROWS, NSEL)
    column = lax.broadcasted_iota(jnp.int32, (SEQS, SEQS), 0)
    slot = lax.broadcasted_iota(jnp.int32, (SEQS, SEQS), 1)
    pair, core = column % PAIRS, column // PAIRS % CORES
    y_hi, place = column // (PAIRS * CORES) % Y_HI, column // (PAIRS * SIDES)
    ordered = jnp.where(batch_index(y_hi, pair, place, core) == slot, 1.0, 0.0)
    wanted = jnp.where(column == assign_ref[...], 1.0, 0.0)
    spots_ref[...] = lax.dot_general(
        ordered, wanted, (((1,), (1,)), ((), ())), preferred_element_type=jnp.float32
    )


def example_grad(both, assign):
    shapes = (
        jax.ShapeDtypeStruct((MEMBERS, ROWS, NSEL), both.dtype),
        jax.ShapeDtypeStruct((SEQS, SEQS), jnp.float32),
    )
    return kernel_call(example_grad_kernel, shapes, (both, assign[None]))


def pairs_kernel(terms_ref, out_ref):
    terms = jnp.swapaxes(terms_ref[...], 0, 1)
    total = jnp.zeros((SEQS, SEQS), jnp.float32)
    for row in range(ROWS):
        total += lax.dot_general(
            terms[row], terms[row], (((1,), (1,)), ((), ())), preferred_element_type=jnp.float32
        )
    for r in range(PLACES):
        for c in range(CORES):
            starts = [((r * Y_HI + y) * CORES + c) * PAIRS for y in range(Y_HI)]
            rows = [total[start : start + PAIRS] for start in starts]
            out_ref[:, r, c, 0] = jnp.concatenate(rows, axis=1)


def pairs(terms):
    shape = jax.ShapeDtypeStruct((PAIRS, PLACES, CORES, 1, Y_HI * SEQS), jnp.float32)
    return kernel_call(pairs_kernel, shape, (terms,))


def side_kernel(rows_ref, out_ref):
    sums = rows_ref[0]
    for member in range(1, DEPTH):
        sums = sums + rows_ref[member]
    for y in range(Y_HI):
        out_ref[y] = jnp.broadcast_to(sums[:, y * SEQS : (y + 1) * SEQS][None], (TENSOR, 1, SEQS))


def place_kernel(rows_ref, spots_ref, out_ref):
    row = rows_ref[0]
    for member in range(1, Y_HI * TENSOR):
        row = row + rows_ref[member]
    norming = 1.0 / (float(TOK) * float(D) * float(NSEL))
    out_ref[...] = lax.dot_general(
        row * norming,
        spots_ref[...],
        (((1,), (0,)), ((), ())),
        precision=lax.Precision.HIGHEST,
        preferred_element_type=jnp.float32,
    )


def on_device(acts, grads, chosen, assign):
    part = selected(chosen, grads)
    shares = lax.all_to_all(part, "tensor", 0, 0, tiled=True)
    both = lax.all_to_all(
        packed(acts, shares), "batch", 0, 0, axis_index_groups=column_groups(), tiled=True
    )
    both = lax.all_to_all(both, "tensor", 0, 0, tiled=True)
    terms, spots = example_grad(both, assign)
    terms = lax.all_to_all(
        terms, ("batch", "tensor"), 0, 0, axis_index_groups=pair_groups(), tiled=True
    )
    rows = pairs(terms).reshape(DEPTH, 1, Y_HI * SEQS)
    rows = lax.all_to_all(rows, "batch", 0, 0, axis_index_groups=depth_groups(), tiled=True)
    shape = jax.ShapeDtypeStruct((Y_HI, TENSOR, 1, SEQS), jnp.float32)
    rows = kernel_call(side_kernel, shape, (rows,)).reshape(Y_HI * TENSOR, 1, SEQS)
    rows = lax.all_to_all(
        rows, ("batch", "tensor"), 0, 0, axis_index_groups=side_groups(), tiled=True
    )
    shape = jax.ShapeDtypeStruct((1, SEQS), jnp.float32)
    return kernel_call(place_kernel, shape, (rows, spots))


def solution(mesh):
    placed = (P("batch", "tensor"), P("batch", "tensor"), P(), P())
    return jax.shard_map(
        on_device, mesh=mesh, in_specs=placed, out_specs=P("batch", None), check_vma=False
    )
```

```python
import jax
import jax.numpy as jnp
from jax import lax
from jax.experimental import pallas as pl
from jax.experimental.pallas import tpu as pltpu
from jax.sharding import PartitionSpec as P

D = 8192
NSEL = 512
TOK = 128
Y_HI, PAIRS, PLACES, CORES = 2, 8, 2, 2
SEQS = Y_HI * PAIRS * PLACES * CORES
SIDES = Y_HI * CORES
DEPTH = PAIRS * PLACES * CORES
Y_LO, X = 2, 4
TENSOR = Y_LO * X
WIDTH = D // TENSOR
PART = WIDTH // PAIRS
HALF = NSEL // Y_LO
TROWS = TOK // X
LANES = 128
BLOCKS = HALF // LANES
PIECE = BLOCKS * TROWS
MEMBERS = PLACES * SIDES * TENSOR
ROWS = WIDTH // MEMBERS
PAIR_OF = (
    (4, 1, 2, 7, 0, 5, 6, 3),
    (3, 7, 1, 5, 2, 6, 0, 4),
    (5, 0, 3, 6, 1, 4, 7, 2),
    (2, 6, 4, 1, 7, 3, 5, 0),
    (6, 2, 5, 0, 3, 7, 4, 1),
    (1, 4, 7, 2, 5, 0, 3, 6),
    (7, 3, 0, 4, 6, 2, 1, 5),
    (0, 5, 6, 3, 4, 1, 2, 7),
)


def batch_index(y_hi, pair, place, core):
    return ((y_hi * PAIRS + pair) * PLACES + place) * CORES + core


def to_pair(block):
    route = [
        (batch_index(y, k, r, c) * TENSOR + t, batch_index(y, PAIR_OF[t][k], r, c) * TENSOR + t)
        for y in range(Y_HI)
        for k in range(PAIRS)
        for r in range(PLACES)
        for c in range(CORES)
        for t in range(TENSOR)
    ]
    return lax.ppermute(block, ("batch", "tensor"), route)


def pair_groups():
    return [
        [
            batch_index(y, k, r, c) * TENSOR + t
            for r in range(PLACES)
            for y in range(Y_HI)
            for c in range(CORES)
            for t in range(TENSOR)
        ]
        for k in range(PAIRS)
    ]


def depth_groups():
    return [
        [batch_index(y, k, r, c) for k in range(PAIRS) for r in range(PLACES) for c in range(CORES)]
        for y in range(Y_HI)
    ]


def side_groups():
    return [
        [batch_index(y, k, r, c) * TENSOR + t for y in range(Y_HI) for t in range(TENSOR)]
        for k in range(PAIRS)
        for r in range(PLACES)
        for c in range(CORES)
    ]


def kernel_call(kernel, out_shape, args, scalars=()):
    smem = pl.BlockSpec(memory_space=pltpu.SMEM)
    vmem = pl.BlockSpec(memory_space=pltpu.VMEM)
    return pl.pallas_call(
        kernel,
        out_shape=out_shape,
        in_specs=[smem] * len(scalars) + [vmem] * len(args),
        out_specs=jax.tree.map(lambda _: vmem, out_shape),
        compiler_params=pltpu.CompilerParams(vmem_limit_bytes=24 * 1024 * 1024),
    )(*scalars, *args)


def chosen_by(number, values):
    found = values[0]
    for i in range(1, len(values)):
        found = jnp.where(number == i, values[i], found)
    return found


def selected(chosen, grads):
    local = chosen - lax.axis_index("tensor") * WIDTH
    places = lax.broadcasted_iota(jnp.int32, (WIDTH, NSEL), 0)
    selector = (places == local[None, :]).astype(grads.dtype)
    return lax.dot_general(
        grads, selector, (((1,), (0,)), ((), ())), preferred_element_type=jnp.float32
    ).astype(grads.dtype)


def pack_kernel(pair_ref, acts_ref, part_ref, out_ref):
    for t in range(TENSOR):
        start = pl.multiple_of(chosen_by(pair_ref[0], PAIR_OF[t]) * PART, PART)
        out_ref[t, :TOK] = acts_ref[:, pl.ds(start, PART)]
        y, x = t // X, t % X
        for j in range(BLOCKS):
            lane = (y * BLOCKS + j) * LANES
            block = part_ref[x * TROWS : (x + 1) * TROWS, lane : lane + LANES]
            out_ref[t, TOK + j * TROWS : TOK + (j + 1) * TROWS] = block


def packed(pair, acts, part):
    shape = jax.ShapeDtypeStruct((TENSOR, TOK + PIECE, LANES), acts.dtype)
    return kernel_call(pack_kernel, shape, (acts, part), (pair,))


def split_kernel(both_ref, acts_ref, copies_ref):
    acts_ref[...] = both_ref[:, :TOK]
    piece = both_ref[0, TOK:].astype(jnp.float32)
    for t in range(1, TENSOR):
        piece = piece + both_ref[t, TOK:].astype(jnp.float32)
    copies_ref[...] = jnp.broadcast_to(piece.astype(copies_ref.dtype)[None], copies_ref.shape)


def split(both):
    shapes = (
        jax.ShapeDtypeStruct((TENSOR, TOK, PART), both.dtype),
        jax.ShapeDtypeStruct((TENSOR, PIECE, LANES), both.dtype),
    )
    return kernel_call(split_kernel, shapes, (both,))


def example_grad_kernel(acts_ref, picked_ref, assign_ref, out_ref, spots_ref):
    blocks = [
        picked_ref[y * X : (y + 1) * X, j * TROWS : (j + 1) * TROWS].reshape(TOK, LANES)
        for y in range(Y_LO)
        for j in range(BLOCKS)
    ]
    picked = jnp.concatenate(blocks, axis=1)
    row = lax.broadcasted_iota(jnp.int32, (PART, NSEL), 0)
    lane = lax.broadcasted_iota(jnp.int32, (PART, NSEL), 1)
    spread = (row * NSEL + lane) * 40503
    count = PART // ROWS
    for t in range(TENSOR):
        grad = lax.dot_general(
            acts_ref[t], picked, (((0,), (0,)), ((), ())), preferred_element_type=jnp.float32
        )
        noise = jnp.bitwise_and(spread + t * 7919, 65535) * 128
        grad = pltpu.stochastic_round(grad, noise.astype(jnp.uint32), target_dtype=out_ref.dtype)
        out_ref[t * count : (t + 1) * count] = grad.reshape(count, ROWS, NSEL)
    column = lax.broadcasted_iota(jnp.int32, (SEQS, SEQS), 0)
    slot = lax.broadcasted_iota(jnp.int32, (SEQS, SEQS), 1)
    pair, core = column % PAIRS, column // PAIRS % CORES
    y_hi, place = column // (PAIRS * CORES) % Y_HI, column // (PAIRS * SIDES)
    ordered = jnp.where(batch_index(y_hi, pair, place, core) == slot, 1.0, 0.0)
    wanted = jnp.where(column == assign_ref[...], 1.0, 0.0)
    spots_ref[...] = lax.dot_general(
        ordered, wanted, (((1,), (1,)), ((), ())), preferred_element_type=jnp.float32
    )


def example_grad(acts, picked, assign):
    shapes = (
        jax.ShapeDtypeStruct((MEMBERS, ROWS, NSEL), acts.dtype),
        jax.ShapeDtypeStruct((SEQS, SEQS), jnp.float32),
    )
    return kernel_call(example_grad_kernel, shapes, (acts, picked, assign[None]))


def pairs_kernel(pair_ref, terms_ref, out_ref):
    terms = jnp.swapaxes(terms_ref[...], 0, 1)
    total = jnp.zeros((SEQS, SEQS), jnp.float32)
    for row in range(ROWS):
        total += lax.dot_general(
            terms[row], terms[row], (((1,), (1,)), ((), ())), preferred_element_type=jnp.float32
        )
    total = total * (1.0 / (float(TOK) * float(D) * float(NSEL)))
    row = lax.broadcasted_iota(jnp.int32, (SEQS, SEQS), 0)
    column = lax.broadcasted_iota(jnp.int32, (SEQS, SEQS), 1)
    held = [chosen_by(pair_ref[0], [PAIR_OF[t].index(k) for k in range(PAIRS)]) for t in range(TENSOR)]
    from_pair = chosen_by(column % TENSOR, held)
    turn = (row // PAIRS == column // TENSOR) & (row % PAIRS == from_pair)
    turn = jnp.where(turn, 1.0, 0.0)
    for side in range(2):
        total = lax.dot_general(
            turn,
            total,
            (((1,), (1,)), ((), ())),
            precision=lax.Precision.HIGHEST,
            preferred_element_type=jnp.float32,
        )
    for r in range(PLACES):
        for c in range(CORES):
            starts = [((r * Y_HI + y) * CORES + c) * PAIRS for y in range(Y_HI)]
            rows = [total[start : start + PAIRS] for start in starts]
            out_ref[:, r, c, 0] = jnp.concatenate(rows, axis=1)


def pairs(pair, terms):
    shape = jax.ShapeDtypeStruct((PAIRS, PLACES, CORES, 1, Y_HI * SEQS), jnp.float32)
    return kernel_call(pairs_kernel, shape, (terms,), (pair,))


def side_kernel(rows_ref, out_ref):
    sums = rows_ref[0]
    for member in range(1, DEPTH):
        sums = sums + rows_ref[member]
    for y in range(Y_HI):
        out_ref[y] = jnp.broadcast_to(sums[:, y * SEQS : (y + 1) * SEQS][None], (TENSOR, 1, SEQS))


def place_kernel(rows_ref, spots_ref, out_ref):
    row = rows_ref[0]
    for member in range(1, Y_HI * TENSOR):
        row = row + rows_ref[member]
    out_ref[...] = lax.dot_general(
        row,
        spots_ref[...],
        (((1,), (0,)), ((), ())),
        precision=lax.Precision.HIGHEST,
        preferred_element_type=jnp.float32,
    )


def on_device(acts, grads, chosen, assign):
    pair = (lax.axis_index("batch") // (PLACES * CORES) % PAIRS)[None]
    both = packed(pair, acts, selected(chosen, grads))
    both = lax.all_to_all(both, "tensor", 0, 0, tiled=True)
    part, copies = split(both)
    part = to_pair(part)
    picked = to_pair(lax.all_to_all(copies, "tensor", 0, 0, tiled=True))
    terms, spots = example_grad(part, picked, assign)
    terms = lax.all_to_all(
        terms, ("batch", "tensor"), 0, 0, axis_index_groups=pair_groups(), tiled=True
    )
    rows = pairs(pair, terms).reshape(DEPTH, 1, Y_HI * SEQS)
    rows = lax.all_to_all(rows, "batch", 0, 0, axis_index_groups=depth_groups(), tiled=True)
    shape = jax.ShapeDtypeStruct((Y_HI, TENSOR, 1, SEQS), jnp.float32)
    rows = kernel_call(side_kernel, shape, (rows,)).reshape(Y_HI * TENSOR, 1, SEQS)
    rows = lax.all_to_all(
        rows, ("batch", "tensor"), 0, 0, axis_index_groups=side_groups(), tiled=True
    )
    shape = jax.ShapeDtypeStruct((1, SEQS), jnp.float32)
    return kernel_call(place_kernel, shape, (rows, spots))


def solution(mesh):
    placed = (P("batch", "tensor"), P("batch", "tensor"), P(), P())
    return jax.shard_map(
        on_device, mesh=mesh, in_specs=placed, out_specs=P("batch", None), check_vma=False
    )
```

```python
import jax
import jax.numpy as jnp
from jax import lax
from jax.experimental import pallas as pl
from jax.experimental.pallas import tpu as pltpu
from jax.sharding import PartitionSpec as P

D = 8192
NSEL = 512
TOK = 128
Y_HI, PAIRS, PLACES, CORES = 2, 8, 2, 2
SEQS = Y_HI * PAIRS * PLACES * CORES
SIDES = Y_HI * CORES
DEPTH = PAIRS * PLACES * CORES
Y_LO, X = 2, 4
TENSOR = Y_LO * X
WIDTH = D // TENSOR
PART = WIDTH // PAIRS
HALF = NSEL // Y_LO
TROWS = TOK // X
LANES = 128
BLOCKS = HALF // LANES
PIECE = BLOCKS * TROWS
MEMBERS = PLACES * SIDES * TENSOR
ROWS = WIDTH // MEMBERS
PAIR_OF = (
    (4, 1, 2, 7, 0, 5, 6, 3),
    (3, 7, 1, 5, 2, 6, 0, 4),
    (5, 0, 3, 6, 1, 4, 7, 2),
    (2, 6, 4, 1, 7, 3, 5, 0),
    (6, 2, 5, 0, 3, 7, 4, 1),
    (1, 4, 7, 2, 5, 0, 3, 6),
    (7, 3, 0, 4, 6, 2, 1, 5),
    (0, 5, 6, 3, 4, 1, 2, 7),
)


def batch_index(y_hi, pair, place, core):
    return ((y_hi * PAIRS + pair) * PLACES + place) * CORES + core


def to_pair(block):
    route = [
        (batch_index(y, k, r, c) * TENSOR + t, batch_index(y, PAIR_OF[t][k], r, c) * TENSOR + t)
        for y in range(Y_HI)
        for k in range(PAIRS)
        for r in range(PLACES)
        for c in range(CORES)
        for t in range(TENSOR)
    ]
    return lax.ppermute(block, ("batch", "tensor"), route)


def pair_groups():
    return [
        [
            batch_index(y, k, r, c) * TENSOR + t
            for r in range(PLACES)
            for y in range(Y_HI)
            for c in range(CORES)
            for t in range(TENSOR)
        ]
        for k in range(PAIRS)
    ]


def depth_groups():
    return [
        [batch_index(y, k, r, c) for k in range(PAIRS) for r in range(PLACES) for c in range(CORES)]
        for y in range(Y_HI)
    ]


def side_groups():
    return [
        [batch_index(y, k, r, c) * TENSOR + t for y in range(Y_HI) for t in range(TENSOR)]
        for k in range(PAIRS)
        for r in range(PLACES)
        for c in range(CORES)
    ]


def kernel_call(kernel, out_shape, args, scalars=()):
    smem = pl.BlockSpec(memory_space=pltpu.SMEM)
    vmem = pl.BlockSpec(memory_space=pltpu.VMEM)
    return pl.pallas_call(
        kernel,
        out_shape=out_shape,
        in_specs=[smem] * len(scalars) + [vmem] * len(args),
        out_specs=jax.tree.map(lambda _: vmem, out_shape),
        compiler_params=pltpu.CompilerParams(vmem_limit_bytes=24 * 1024 * 1024),
    )(*scalars, *args)


def chosen_by(number, values):
    found = values[0]
    for i in range(1, len(values)):
        found = jnp.where(number == i, values[i], found)
    return found


def selected(chosen, grads):
    local = chosen - lax.axis_index("tensor") * WIDTH
    places = lax.broadcasted_iota(jnp.int32, (WIDTH, NSEL), 0)
    selector = (places == local[None, :]).astype(grads.dtype)
    return lax.dot_general(
        grads, selector, (((1,), (0,)), ((), ())), preferred_element_type=jnp.float32
    ).astype(grads.dtype)


def pack_kernel(pair_ref, acts_ref, part_ref, out_ref):
    for t in range(TENSOR):
        start = pl.multiple_of(chosen_by(pair_ref[0], PAIR_OF[t]) * PART, PART)
        out_ref[t, :TOK] = acts_ref[:, pl.ds(start, PART)]
        y, x = t // X, t % X
        for j in range(BLOCKS):
            lane = (y * BLOCKS + j) * LANES
            block = part_ref[x * TROWS : (x + 1) * TROWS, lane : lane + LANES]
            out_ref[t, TOK + j * TROWS : TOK + (j + 1) * TROWS] = block


def packed(pair, acts, part):
    shape = jax.ShapeDtypeStruct((TENSOR, TOK + PIECE, LANES), acts.dtype)
    return kernel_call(pack_kernel, shape, (acts, part), (pair,))


def split_kernel(both_ref, acts_ref, copies_ref):
    acts_ref[...] = both_ref[:, :TOK]
    piece = both_ref[0, TOK:].astype(jnp.float32)
    for t in range(1, TENSOR):
        piece = piece + both_ref[t, TOK:].astype(jnp.float32)
    copies_ref[...] = jnp.broadcast_to(piece.astype(copies_ref.dtype)[None], copies_ref.shape)


def split(both):
    shapes = (
        jax.ShapeDtypeStruct((TENSOR, TOK, PART), both.dtype),
        jax.ShapeDtypeStruct((TENSOR, PIECE, LANES), both.dtype),
    )
    return kernel_call(split_kernel, shapes, (both,))


def example_grad_kernel(acts_ref, picked_ref, assign_ref, out_ref, spots_ref):
    blocks = [
        picked_ref[y * X : (y + 1) * X, j * TROWS : (j + 1) * TROWS].reshape(TOK, LANES)
        for y in range(Y_LO)
        for j in range(BLOCKS)
    ]
    picked = jnp.concatenate(blocks, axis=1)
    row = lax.broadcasted_iota(jnp.int32, (PART, NSEL), 0)
    lane = lax.broadcasted_iota(jnp.int32, (PART, NSEL), 1)
    spread = (row * NSEL + lane) * 40503
    count = PART // ROWS
    for t in range(TENSOR):
        grad = lax.dot_general(
            acts_ref[t], picked, (((0,), (0,)), ((), ())), preferred_element_type=jnp.float32
        )
        noise = jnp.bitwise_and(spread + t * 7919, 65535) * 128
        grad = pltpu.stochastic_round(grad, noise.astype(jnp.uint32), target_dtype=out_ref.dtype)
        out_ref[t * count : (t + 1) * count] = grad.reshape(count, ROWS, NSEL)
    column = lax.broadcasted_iota(jnp.int32, (SEQS, SEQS), 0)
    slot = lax.broadcasted_iota(jnp.int32, (SEQS, SEQS), 1)
    pair, core = column % PAIRS, column // PAIRS % CORES
    y_hi, place = column // (PAIRS * CORES) % Y_HI, column // (PAIRS * SIDES)
    ordered = jnp.where(batch_index(y_hi, pair, place, core) == slot, 1.0, 0.0)
    wanted = jnp.where(column == assign_ref[...], 1.0, 0.0)
    spots_ref[...] = lax.dot_general(
        ordered, wanted, (((1,), (1,)), ((), ())), preferred_element_type=jnp.float32
    )


def example_grad(acts, picked, assign):
    shapes = (
        jax.ShapeDtypeStruct((MEMBERS, ROWS, NSEL), acts.dtype),
        jax.ShapeDtypeStruct((SEQS, SEQS), jnp.float32),
    )
    return kernel_call(example_grad_kernel, shapes, (acts, picked, assign[None]))


def pairs_kernel(pair_ref, terms_ref, out_ref):
    terms = jnp.swapaxes(terms_ref[...], 0, 1)
    total = jnp.zeros((SEQS, SEQS), jnp.float32)
    for row in range(ROWS):
        total += lax.dot_general(
            terms[row], terms[row], (((1,), (1,)), ((), ())), preferred_element_type=jnp.float32
        )
    total = total * (1.0 / (float(TOK) * float(D) * float(NSEL)))
    held = [chosen_by(pair_ref[0], [PAIR_OF[t].index(k) for k in range(PAIRS)]) for t in range(TENSOR)]
    row = lax.broadcasted_iota(jnp.int32, (SEQS, SEQS), 0)
    column = lax.broadcasted_iota(jnp.int32, (SEQS, SEQS), 1)
    tensor = jnp.bitwise_and(lax.broadcasted_iota(jnp.int32, (1, SEQS), 1), TENSOR - 1)
    source = jnp.bitwise_and(column, ~(TENSOR - 1)) + chosen_by(tensor, held)
    total = lax.dot_general(
        total,
        jnp.where(row == source, 1.0, 0.0),
        (((1,), (1,)), ((), ())),
        precision=lax.Precision.HIGHEST,
        preferred_element_type=jnp.float32,
    )
    for r in range(PLACES):
        for c in range(CORES):
            starts = [((r * Y_HI + y) * CORES + c) * TENSOR for y in range(Y_HI)]
            rows = jnp.concatenate([total[start : start + TENSOR] for start in starts], axis=1)
            for t in range(TENSOR):
                out_ref[pl.ds(held[t], 1), r, c] = rows[t : t + 1][None]


def pairs(pair, terms):
    shape = jax.ShapeDtypeStruct((PAIRS, PLACES, CORES, 1, Y_HI * SEQS), jnp.float32)
    return kernel_call(pairs_kernel, shape, (terms,), (pair,))


def side_kernel(rows_ref, out_ref):
    sums = rows_ref[0]
    for member in range(1, DEPTH):
        sums = sums + rows_ref[member]
    for y in range(Y_HI):
        out_ref[y] = jnp.broadcast_to(sums[:, y * SEQS : (y + 1) * SEQS][None], (TENSOR, 1, SEQS))


def place_kernel(rows_ref, spots_ref, out_ref):
    row = rows_ref[0]
    for member in range(1, Y_HI * TENSOR):
        row = row + rows_ref[member]
    out_ref[...] = lax.dot_general(
        row,
        spots_ref[...],
        (((1,), (0,)), ((), ())),
        precision=lax.Precision.HIGHEST,
        preferred_element_type=jnp.float32,
    )


def on_device(acts, grads, chosen, assign):
    pair = (lax.axis_index("batch") // (PLACES * CORES) % PAIRS)[None]
    both = packed(pair, acts, selected(chosen, grads))
    both = lax.all_to_all(both, "tensor", 0, 0, tiled=True)
    part, copies = split(both)
    part = to_pair(part)
    picked = to_pair(lax.all_to_all(copies, "tensor", 0, 0, tiled=True))
    terms, spots = example_grad(part, picked, assign)
    terms = lax.all_to_all(
        terms, ("batch", "tensor"), 0, 0, axis_index_groups=pair_groups(), tiled=True
    )
    rows = pairs(pair, terms).reshape(DEPTH, 1, Y_HI * SEQS)
    rows = lax.all_to_all(rows, "batch", 0, 0, axis_index_groups=depth_groups(), tiled=True)
    shape = jax.ShapeDtypeStruct((Y_HI, TENSOR, 1, SEQS), jnp.float32)
    rows = kernel_call(side_kernel, shape, (rows,)).reshape(Y_HI * TENSOR, 1, SEQS)
    rows = lax.all_to_all(
        rows, ("batch", "tensor"), 0, 0, axis_index_groups=side_groups(), tiled=True
    )
    shape = jax.ShapeDtypeStruct((1, SEQS), jnp.float32)
    return kernel_call(place_kernel, shape, (rows, spots))


def solution(mesh):
    placed = (P("batch", "tensor"), P("batch", "tensor"), P(), P())
    return jax.shard_map(
        on_device, mesh=mesh, in_specs=placed, out_specs=P("batch", None), check_vma=False
    )
```

```python
import jax
import jax.numpy as jnp
from jax import lax
from jax.experimental import pallas as pl
from jax.experimental.pallas import tpu as pltpu
from jax.sharding import PartitionSpec as P

D = 8192
NSEL = 512
TOK = 128
Y_HI, PAIRS, PLACES, CORES = 2, 8, 2, 2
SEQS = Y_HI * PAIRS * PLACES * CORES
SIDES = Y_HI * CORES
DEPTH = PAIRS * PLACES * CORES
Y_LO, X = 2, 4
TENSOR = Y_LO * X
WIDTH = D // TENSOR
PART = WIDTH // PAIRS
HALF = NSEL // Y_LO
TROWS = TOK // X
LANES = 128
BLOCKS = HALF // LANES
PIECE = BLOCKS * TROWS
MEMBERS = PLACES * SIDES * TENSOR
ROWS = WIDTH // MEMBERS
PAIR_OF = (
    (4, 1, 2, 7, 0, 5, 6, 3),
    (3, 7, 1, 5, 2, 6, 0, 4),
    (5, 0, 3, 6, 1, 4, 7, 2),
    (2, 6, 4, 1, 7, 3, 5, 0),
    (6, 2, 5, 0, 3, 7, 4, 1),
    (1, 4, 7, 2, 5, 0, 3, 6),
    (7, 3, 0, 4, 6, 2, 1, 5),
    (0, 5, 6, 3, 4, 1, 2, 7),
)


def batch_index(y_hi, pair, place, core):
    return ((y_hi * PAIRS + pair) * PLACES + place) * CORES + core


def to_pair(block):
    route = [
        (batch_index(y, k, r, c) * TENSOR + t, batch_index(y, PAIR_OF[t][k], r, c) * TENSOR + t)
        for y in range(Y_HI)
        for k in range(PAIRS)
        for r in range(PLACES)
        for c in range(CORES)
        for t in range(TENSOR)
    ]
    return lax.ppermute(block, ("batch", "tensor"), route)


def pair_groups():
    return [
        [
            batch_index(y, k, r, c) * TENSOR + t
            for r in range(PLACES)
            for y in range(Y_HI)
            for c in range(CORES)
            for t in range(TENSOR)
        ]
        for k in range(PAIRS)
    ]


def depth_groups():
    return [
        [batch_index(y, k, r, c) for k in range(PAIRS) for r in range(PLACES) for c in range(CORES)]
        for y in range(Y_HI)
    ]


def side_groups():
    return [
        [batch_index(y, k, r, c) * TENSOR + t for y in range(Y_HI) for t in range(TENSOR)]
        for k in range(PAIRS)
        for r in range(PLACES)
        for c in range(CORES)
    ]


def kernel_call(kernel, out_shape, args, scalars=()):
    smem = pl.BlockSpec(memory_space=pltpu.SMEM)
    vmem = pl.BlockSpec(memory_space=pltpu.VMEM)
    return pl.pallas_call(
        kernel,
        out_shape=out_shape,
        in_specs=[smem] * len(scalars) + [vmem] * len(args),
        out_specs=jax.tree.map(lambda _: vmem, out_shape),
        compiler_params=pltpu.CompilerParams(vmem_limit_bytes=24 * 1024 * 1024),
    )(*scalars, *args)


def chosen_by(number, values):
    found = values[0]
    for i in range(1, len(values)):
        found = jnp.where(number == i, values[i], found)
    return found


def selected(chosen, grads):
    local = chosen - lax.axis_index("tensor") * WIDTH
    places = lax.broadcasted_iota(jnp.int32, (WIDTH, NSEL), 0)
    selector = (places == local[None, :]).astype(grads.dtype)
    return lax.dot_general(
        grads, selector, (((1,), (0,)), ((), ())), preferred_element_type=jnp.float32
    ).astype(grads.dtype)


def pack_kernel(pair_ref, acts_ref, part_ref, out_ref):
    for t in range(TENSOR):
        start = pl.multiple_of(chosen_by(pair_ref[0], PAIR_OF[t]) * PART, PART)
        out_ref[t, :TOK] = acts_ref[:, pl.ds(start, PART)]
        y, x = t // X, t % X
        for j in range(BLOCKS):
            lane = (y * BLOCKS + j) * LANES
            block = part_ref[x * TROWS : (x + 1) * TROWS, lane : lane + LANES]
            out_ref[t, TOK + j * TROWS : TOK + (j + 1) * TROWS] = block


def packed(pair, acts, part):
    shape = jax.ShapeDtypeStruct((TENSOR, TOK + PIECE, LANES), acts.dtype)
    return kernel_call(pack_kernel, shape, (acts, part), (pair,))


def split_kernel(both_ref, acts_ref, copies_ref):
    acts_ref[...] = both_ref[:, :TOK]
    piece = both_ref[0, TOK:].astype(jnp.float32)
    for t in range(1, TENSOR):
        piece = piece + both_ref[t, TOK:].astype(jnp.float32)
    copies_ref[...] = jnp.broadcast_to(piece.astype(copies_ref.dtype)[None], copies_ref.shape)


def split(both):
    shapes = (
        jax.ShapeDtypeStruct((TENSOR, TOK, PART), both.dtype),
        jax.ShapeDtypeStruct((TENSOR, PIECE, LANES), both.dtype),
    )
    return kernel_call(split_kernel, shapes, (both,))


def example_grad_kernel(acts_ref, picked_ref, assign_ref, out_ref, spots_ref):
    blocks = [
        picked_ref[y * X : (y + 1) * X, j * TROWS : (j + 1) * TROWS].reshape(TOK, LANES)
        for y in range(Y_LO)
        for j in range(BLOCKS)
    ]
    picked = jnp.concatenate(blocks, axis=1)
    row = lax.broadcasted_iota(jnp.int32, (PART, NSEL), 0)
    lane = lax.broadcasted_iota(jnp.int32, (PART, NSEL), 1)
    spread = (row * NSEL + lane) * 40503
    count = PART // ROWS
    for t in range(TENSOR):
        grad = lax.dot_general(
            acts_ref[t], picked, (((0,), (0,)), ((), ())), preferred_element_type=jnp.float32
        )
        noise = jnp.bitwise_and(spread + t * 7919, 65535) * 128
        grad = pltpu.stochastic_round(grad, noise.astype(jnp.uint32), target_dtype=out_ref.dtype)
        out_ref[t * count : (t + 1) * count] = grad.reshape(count, ROWS, NSEL)
    column = lax.broadcasted_iota(jnp.int32, (SEQS, SEQS), 0)
    slot = lax.broadcasted_iota(jnp.int32, (SEQS, SEQS), 1)
    pair, core = column % PAIRS, column // PAIRS % CORES
    y_hi, place = column // (PAIRS * CORES) % Y_HI, column // (PAIRS * SIDES)
    ordered = jnp.where(batch_index(y_hi, pair, place, core) == slot, 1.0, 0.0)
    wanted = jnp.where(column == assign_ref[...], 1.0, 0.0)
    spots_ref[...] = lax.dot_general(
        ordered, wanted, (((1,), (1,)), ((), ())), preferred_element_type=jnp.float32
    )


def example_grad(acts, picked, assign):
    shapes = (
        jax.ShapeDtypeStruct((MEMBERS, ROWS, NSEL), acts.dtype),
        jax.ShapeDtypeStruct((SEQS, SEQS), jnp.float32),
    )
    return kernel_call(example_grad_kernel, shapes, (acts, picked, assign[None]))


def pairs_kernel(pair_ref, terms_ref, out_ref):
    terms = jnp.swapaxes(terms_ref[...], 0, 1)
    total = jnp.zeros((SEQS, SEQS), jnp.float32)
    for row in range(ROWS):
        total += lax.dot_general(
            terms[row], terms[row], (((1,), (1,)), ((), ())), preferred_element_type=jnp.float32
        )
    total = total * (1.0 / (float(TOK) * float(D) * float(NSEL)))
    held = [chosen_by(pair_ref[0], [PAIR_OF[t].index(k) for k in range(PAIRS)]) for t in range(TENSOR)]
    row = lax.broadcasted_iota(jnp.int32, (SEQS, SEQS), 0)
    column = lax.broadcasted_iota(jnp.int32, (SEQS, SEQS), 1)
    tensor = jnp.bitwise_and(lax.broadcasted_iota(jnp.int32, (1, SEQS), 1), TENSOR - 1)
    source = jnp.bitwise_and(column, ~(TENSOR - 1)) + chosen_by(tensor, held)
    total = lax.dot_general(
        total,
        jnp.where(row == source, 1.0, 0.0),
        (((1,), (1,)), ((), ())),
        precision=lax.Precision.HIGHEST,
        preferred_element_type=jnp.float32,
    )
    for r in range(PLACES):
        for c in range(CORES):
            starts = [((r * Y_HI + y) * CORES + c) * TENSOR for y in range(Y_HI)]
            rows = jnp.concatenate([total[start : start + TENSOR] for start in starts], axis=1)
            for t in range(TENSOR):
                out_ref[pl.ds(held[t], 1), r, c] = rows[t : t + 1][None]


def pairs(pair, terms):
    shape = jax.ShapeDtypeStruct((PAIRS, PLACES, CORES, 1, Y_HI * SEQS), jnp.float32)
    return kernel_call(pairs_kernel, shape, (terms,), (pair,))


def side_kernel(rows_ref, out_ref):
    sums = rows_ref[0]
    for member in range(1, DEPTH):
        sums = sums + rows_ref[member]
    for y in range(Y_HI):
        out_ref[y] = jnp.broadcast_to(sums[:, y * SEQS : (y + 1) * SEQS][None], (TENSOR, 1, SEQS))


def place_kernel(rows_ref, spots_ref, out_ref):
    row = rows_ref[0]
    for member in range(1, Y_HI * TENSOR):
        row = row + rows_ref[member]
    out_ref[...] = lax.dot_general(
        row,
        spots_ref[...],
        (((1,), (0,)), ((), ())),
        precision=lax.Precision.HIGHEST,
        preferred_element_type=jnp.float32,
    )


def on_device(acts, grads, chosen, assign):
    pair = (lax.axis_index("batch") // (PLACES * CORES) % PAIRS)[None]
    both = packed(pair, acts, selected(chosen, grads))
    both = lax.all_to_all(both, "tensor", 0, 0, tiled=True)
    part, copies = split(both)
    picked = lax.all_to_all(copies, "tensor", 0, 0, tiled=True)
    part, picked = lax.optimization_barrier((part, picked))
    part, picked = to_pair(part), to_pair(picked)
    terms, spots = example_grad(part, picked, assign)
    terms = lax.all_to_all(
        terms, ("batch", "tensor"), 0, 0, axis_index_groups=pair_groups(), tiled=True
    )
    rows = pairs(pair, terms).reshape(DEPTH, 1, Y_HI * SEQS)
    rows = lax.all_to_all(rows, "batch", 0, 0, axis_index_groups=depth_groups(), tiled=True)
    shape = jax.ShapeDtypeStruct((Y_HI, TENSOR, 1, SEQS), jnp.float32)
    rows = kernel_call(side_kernel, shape, (rows,)).reshape(Y_HI * TENSOR, 1, SEQS)
    rows = lax.all_to_all(
        rows, ("batch", "tensor"), 0, 0, axis_index_groups=side_groups(), tiled=True
    )
    shape = jax.ShapeDtypeStruct((1, SEQS), jnp.float32)
    return kernel_call(place_kernel, shape, (rows, spots))


def solution(mesh):
    placed = (P("batch", "tensor"), P("batch", "tensor"), P(), P())
    return jax.shard_map(
        on_device, mesh=mesh, in_specs=placed, out_specs=P("batch", None), check_vma=False
    )
```

```python
import jax
import jax.numpy as jnp
from jax import lax
from jax.experimental import pallas as pl
from jax.experimental.pallas import tpu as pltpu
from jax.sharding import PartitionSpec as P

D = 8192
NSEL = 512
TOK = 128
Y_HI, PAIRS, PLACES, CORES = 2, 8, 2, 2
SEQS = Y_HI * PAIRS * PLACES * CORES
SIDES = Y_HI * CORES
DEPTH = PAIRS * PLACES * CORES
Y_LO, X = 2, 4
TENSOR = Y_LO * X
WIDTH = D // TENSOR
PART = WIDTH // PAIRS
HALF = NSEL // Y_LO
TROWS = TOK // X
LANES = 128
BLOCKS = HALF // LANES
PIECE = BLOCKS * TROWS
REPEATS = 2
MEMBERS = PLACES * SIDES * TENSOR
ROWS = WIDTH // MEMBERS
PAIR_OF = (
    (4, 1, 2, 7, 0, 5, 6, 3),
    (3, 7, 1, 5, 2, 6, 0, 4),
    (5, 0, 3, 6, 1, 4, 7, 2),
    (2, 6, 4, 1, 7, 3, 5, 0),
    (6, 2, 5, 0, 3, 7, 4, 1),
    (1, 4, 7, 2, 5, 0, 3, 6),
    (7, 3, 0, 4, 6, 2, 1, 5),
    (0, 5, 6, 3, 4, 1, 2, 7),
)


def batch_index(y_hi, pair, place, core):
    return ((y_hi * PAIRS + pair) * PLACES + place) * CORES + core


def to_pair(block):
    route = [
        (batch_index(y, k, r, c) * TENSOR + t, batch_index(y, PAIR_OF[t][k], r, c) * TENSOR + t)
        for y in range(Y_HI)
        for k in range(PAIRS)
        for r in range(PLACES)
        for c in range(CORES)
        for t in range(TENSOR)
    ]
    return lax.ppermute(block, ("batch", "tensor"), route)


def pair_groups():
    return [
        [
            batch_index(y, k, r, c) * TENSOR + t
            for r in range(PLACES)
            for y in range(Y_HI)
            for c in range(CORES)
            for t in range(TENSOR)
        ]
        for k in range(PAIRS)
    ]


def depth_groups():
    return [
        [batch_index(y, k, r, c) for k in range(PAIRS) for r in range(PLACES) for c in range(CORES)]
        for y in range(Y_HI)
    ]


def side_groups():
    return [
        [batch_index(y, k, r, c) * TENSOR + t for y in range(Y_HI) for t in range(TENSOR)]
        for k in range(PAIRS)
        for r in range(PLACES)
        for c in range(CORES)
    ]


def kernel_call(kernel, out_shape, args, scalars=()):
    smem = pl.BlockSpec(memory_space=pltpu.SMEM)
    vmem = pl.BlockSpec(memory_space=pltpu.VMEM)
    return pl.pallas_call(
        kernel,
        out_shape=out_shape,
        in_specs=[smem] * len(scalars) + [vmem] * len(args),
        out_specs=jax.tree.map(lambda _: vmem, out_shape),
        compiler_params=pltpu.CompilerParams(vmem_limit_bytes=24 * 1024 * 1024),
    )(*scalars, *args)


def chosen_by(number, values):
    found = values[0]
    for i in range(1, len(values)):
        found = jnp.where(number == i, values[i], found)
    return found


def selected(chosen, grads):
    local = chosen - lax.axis_index("tensor") * WIDTH
    places = lax.broadcasted_iota(jnp.int32, (WIDTH, NSEL), 0)
    selector = (places == local[None, :]).astype(grads.dtype)
    return lax.dot_general(
        grads, selector, (((1,), (0,)), ((), ())), preferred_element_type=jnp.float32
    ).astype(grads.dtype)


def pack_kernel(pair_ref, acts_ref, part_ref, out_ref):
    for t in range(TENSOR):
        start = pl.multiple_of(chosen_by(pair_ref[0], PAIR_OF[t]) * PART, PART)
        out_ref[t, :TOK] = acts_ref[:, pl.ds(start, PART)]
        y, x = t // X, t % X
        for j in range(BLOCKS):
            lane = (y * BLOCKS + j) * LANES
            block = part_ref[x * TROWS : (x + 1) * TROWS, lane : lane + LANES]
            out_ref[t, TOK + j * TROWS : TOK + (j + 1) * TROWS] = block


def packed(pair, acts, part):
    shape = jax.ShapeDtypeStruct((TENSOR, TOK + PIECE, LANES), acts.dtype)
    return kernel_call(pack_kernel, shape, (acts, part), (pair,))


def split_kernel(both_ref, acts_ref, copies_ref):
    acts_ref[...] = both_ref[:, :TOK]
    piece = both_ref[0, TOK:].astype(jnp.float32)
    for t in range(1, TENSOR):
        piece = piece + both_ref[t, TOK:].astype(jnp.float32)
    piece = piece.astype(copies_ref.dtype)
    for t in range(TENSOR):
        for i in range(REPEATS):
            copies_ref[t, i * PIECE : (i + 1) * PIECE] = piece


def split(both):
    shapes = (
        jax.ShapeDtypeStruct((TENSOR, TOK, PART), both.dtype),
        jax.ShapeDtypeStruct((TENSOR, REPEATS * PIECE, LANES), both.dtype),
    )
    return kernel_call(split_kernel, shapes, (both,))


def example_grad_kernel(acts_ref, picked_ref, assign_ref, out_ref, spots_ref):
    blocks = [
        picked_ref[y * X : (y + 1) * X, j * TROWS : (j + 1) * TROWS].reshape(TOK, LANES)
        for y in range(Y_LO)
        for j in range(BLOCKS)
    ]
    picked = jnp.concatenate(blocks, axis=1)
    row = lax.broadcasted_iota(jnp.int32, (PART, NSEL), 0)
    lane = lax.broadcasted_iota(jnp.int32, (PART, NSEL), 1)
    spread = (row * NSEL + lane) * 40503
    count = PART // ROWS
    for t in range(TENSOR):
        grad = lax.dot_general(
            acts_ref[t], picked, (((0,), (0,)), ((), ())), preferred_element_type=jnp.float32
        )
        noise = jnp.bitwise_and(spread + t * 7919, 65535) * 128
        grad = pltpu.stochastic_round(grad, noise.astype(jnp.uint32), target_dtype=out_ref.dtype)
        out_ref[t * count : (t + 1) * count] = grad.reshape(count, ROWS, NSEL)
    column = lax.broadcasted_iota(jnp.int32, (SEQS, SEQS), 0)
    slot = lax.broadcasted_iota(jnp.int32, (SEQS, SEQS), 1)
    pair, core = column % PAIRS, column // PAIRS % CORES
    y_hi, place = column // (PAIRS * CORES) % Y_HI, column // (PAIRS * SIDES)
    ordered = jnp.where(batch_index(y_hi, pair, place, core) == slot, 1.0, 0.0)
    wanted = jnp.where(column == assign_ref[...], 1.0, 0.0)
    spots_ref[...] = lax.dot_general(
        ordered, wanted, (((1,), (1,)), ((), ())), preferred_element_type=jnp.float32
    )


def example_grad(acts, picked, assign):
    shapes = (
        jax.ShapeDtypeStruct((MEMBERS, ROWS, NSEL), acts.dtype),
        jax.ShapeDtypeStruct((SEQS, SEQS), jnp.float32),
    )
    return kernel_call(example_grad_kernel, shapes, (acts, picked, assign[None]))


def pairs_kernel(pair_ref, terms_ref, out_ref):
    terms = jnp.swapaxes(terms_ref[...], 0, 1)
    total = jnp.zeros((SEQS, SEQS), jnp.float32)
    for row in range(ROWS):
        total += lax.dot_general(
            terms[row], terms[row], (((1,), (1,)), ((), ())), preferred_element_type=jnp.float32
        )
    total = total * (1.0 / (float(TOK) * float(D) * float(NSEL)))
    held = [chosen_by(pair_ref[0], [PAIR_OF[t].index(k) for k in range(PAIRS)]) for t in range(TENSOR)]
    row = lax.broadcasted_iota(jnp.int32, (SEQS, SEQS), 0)
    column = lax.broadcasted_iota(jnp.int32, (SEQS, SEQS), 1)
    tensor = jnp.bitwise_and(lax.broadcasted_iota(jnp.int32, (1, SEQS), 1), TENSOR - 1)
    source = jnp.bitwise_and(column, ~(TENSOR - 1)) + chosen_by(tensor, held)
    total = lax.dot_general(
        total,
        jnp.where(row == source, 1.0, 0.0),
        (((1,), (1,)), ((), ())),
        precision=lax.Precision.HIGHEST,
        preferred_element_type=jnp.float32,
    )
    for r in range(PLACES):
        for c in range(CORES):
            starts = [((r * Y_HI + y) * CORES + c) * TENSOR for y in range(Y_HI)]
            rows = jnp.concatenate([total[start : start + TENSOR] for start in starts], axis=1)
            for t in range(TENSOR):
                out_ref[pl.ds(held[t], 1), r, c] = rows[t : t + 1][None]


def pairs(pair, terms):
    shape = jax.ShapeDtypeStruct((PAIRS, PLACES, CORES, 1, Y_HI * SEQS), jnp.float32)
    return kernel_call(pairs_kernel, shape, (terms,), (pair,))


def side_kernel(rows_ref, out_ref):
    sums = rows_ref[0]
    for member in range(1, DEPTH):
        sums = sums + rows_ref[member]
    for y in range(Y_HI):
        out_ref[y] = jnp.broadcast_to(sums[:, y * SEQS : (y + 1) * SEQS][None], (TENSOR, 1, SEQS))


def place_kernel(rows_ref, spots_ref, out_ref):
    row = rows_ref[0]
    for member in range(1, Y_HI * TENSOR):
        row = row + rows_ref[member]
    out_ref[...] = lax.dot_general(
        row,
        spots_ref[...],
        (((1,), (0,)), ((), ())),
        precision=lax.Precision.HIGHEST,
        preferred_element_type=jnp.float32,
    )


def on_device(acts, grads, chosen, assign):
    pair = (lax.axis_index("batch") // (PLACES * CORES) % PAIRS)[None]
    both = packed(pair, acts, selected(chosen, grads))
    both = lax.all_to_all(both, "tensor", 0, 0, tiled=True)
    part, copies = split(both)
    part = to_pair(part)
    picked = to_pair(lax.all_to_all(copies, "tensor", 0, 0, tiled=True)[:, :PIECE])
    terms, spots = example_grad(part, picked, assign)
    terms = lax.all_to_all(
        terms, ("batch", "tensor"), 0, 0, axis_index_groups=pair_groups(), tiled=True
    )
    rows = pairs(pair, terms).reshape(DEPTH, 1, Y_HI * SEQS)
    rows = lax.all_to_all(rows, "batch", 0, 0, axis_index_groups=depth_groups(), tiled=True)
    shape = jax.ShapeDtypeStruct((Y_HI, TENSOR, 1, SEQS), jnp.float32)
    rows = kernel_call(side_kernel, shape, (rows,)).reshape(Y_HI * TENSOR, 1, SEQS)
    rows = lax.all_to_all(
        rows, ("batch", "tensor"), 0, 0, axis_index_groups=side_groups(), tiled=True
    )
    shape = jax.ShapeDtypeStruct((1, SEQS), jnp.float32)
    return kernel_call(place_kernel, shape, (rows, spots))


def solution(mesh):
    placed = (P("batch", "tensor"), P("batch", "tensor"), P(), P())
    return jax.shard_map(
        on_device, mesh=mesh, in_specs=placed, out_specs=P("batch", None), check_vma=False
    )
```

```python
import jax
import jax.numpy as jnp
from jax import lax
from jax.experimental import pallas as pl
from jax.experimental.pallas import tpu as pltpu
from jax.sharding import PartitionSpec as P

D = 8192
NSEL = 512
TOK = 128
Y_HI, PAIRS, PLACES, CORES = 2, 8, 2, 2
SEQS = Y_HI * PAIRS * PLACES * CORES
SIDES = Y_HI * CORES
DEPTH = PAIRS * PLACES * CORES
Y_LO, X = 2, 4
TENSOR = Y_LO * X
WIDTH = D // TENSOR
PART = WIDTH // PAIRS
HALF = NSEL // Y_LO
TROWS = TOK // X
LANES = 128
BLOCKS = HALF // LANES
PIECE = BLOCKS * TROWS
MEMBERS = PLACES * SIDES * TENSOR
ROWS = WIDTH // MEMBERS
PAIR_OF = (
    (4, 1, 2, 7, 0, 5, 6, 3),
    (3, 7, 1, 5, 2, 6, 0, 4),
    (5, 0, 3, 6, 1, 4, 7, 2),
    (2, 6, 4, 1, 7, 3, 5, 0),
    (6, 2, 5, 0, 3, 7, 4, 1),
    (1, 4, 7, 2, 5, 0, 3, 6),
    (7, 3, 0, 4, 6, 2, 1, 5),
    (0, 5, 6, 3, 4, 1, 2, 7),
)


def batch_index(y_hi, pair, place, core):
    return ((y_hi * PAIRS + pair) * PLACES + place) * CORES + core


def to_pair(block):
    route = [
        (batch_index(y, k, r, c) * TENSOR + t, batch_index(y, PAIR_OF[t][k], r, c) * TENSOR + t)
        for y in range(Y_HI)
        for k in range(PAIRS)
        for r in range(PLACES)
        for c in range(CORES)
        for t in range(TENSOR)
    ]
    return lax.ppermute(block, ("batch", "tensor"), route)


def pair_groups():
    held_by = [
        [next(t for t in range(TENSOR) if PAIR_OF[t][k] == pair) for k in range(PAIRS)]
        for pair in range(PAIRS)
    ]
    return [
        [
            batch_index(y, pair, r, c) * TENSOR + held_by[pair][k]
            for r in range(PLACES)
            for y in range(Y_HI)
            for c in range(CORES)
            for k in range(PAIRS)
        ]
        for pair in range(PAIRS)
    ]


def depth_groups():
    return [
        [batch_index(y, k, r, c) for k in range(PAIRS) for r in range(PLACES) for c in range(CORES)]
        for y in range(Y_HI)
    ]


def side_groups():
    return [
        [batch_index(y, k, r, c) * TENSOR + t for y in range(Y_HI) for t in range(TENSOR)]
        for k in range(PAIRS)
        for r in range(PLACES)
        for c in range(CORES)
    ]


def kernel_call(kernel, out_shape, args, scalars=()):
    smem = pl.BlockSpec(memory_space=pltpu.SMEM)
    vmem = pl.BlockSpec(memory_space=pltpu.VMEM)
    return pl.pallas_call(
        kernel,
        out_shape=out_shape,
        in_specs=[smem] * len(scalars) + [vmem] * len(args),
        out_specs=jax.tree.map(lambda _: vmem, out_shape),
        compiler_params=pltpu.CompilerParams(vmem_limit_bytes=24 * 1024 * 1024),
    )(*scalars, *args)


def chosen_by(number, values):
    found = values[0]
    for i in range(1, len(values)):
        found = jnp.where(number == i, values[i], found)
    return found


def selected(chosen, grads):
    local = chosen - lax.axis_index("tensor") * WIDTH
    places = lax.broadcasted_iota(jnp.int32, (WIDTH, NSEL), 0)
    selector = (places == local[None, :]).astype(grads.dtype)
    return lax.dot_general(
        grads, selector, (((1,), (0,)), ((), ())), preferred_element_type=jnp.float32
    ).astype(grads.dtype)


def pack_kernel(pair_ref, acts_ref, part_ref, out_ref):
    for t in range(TENSOR):
        start = pl.multiple_of(chosen_by(pair_ref[0], PAIR_OF[t]) * PART, PART)
        out_ref[t, :TOK] = acts_ref[:, pl.ds(start, PART)]
        y, x = t // X, t % X
        for j in range(BLOCKS):
            lane = (y * BLOCKS + j) * LANES
            block = part_ref[x * TROWS : (x + 1) * TROWS, lane : lane + LANES]
            out_ref[t, TOK + j * TROWS : TOK + (j + 1) * TROWS] = block


def packed(pair, acts, part):
    shape = jax.ShapeDtypeStruct((TENSOR, TOK + PIECE, LANES), acts.dtype)
    return kernel_call(pack_kernel, shape, (acts, part), (pair,))


def split_kernel(both_ref, acts_ref, copies_ref):
    acts_ref[...] = both_ref[:, :TOK]
    piece = both_ref[0, TOK:].astype(jnp.float32)
    for t in range(1, TENSOR):
        piece = piece + both_ref[t, TOK:].astype(jnp.float32)
    copies_ref[...] = jnp.broadcast_to(piece.astype(copies_ref.dtype)[None], copies_ref.shape)


def split(both):
    shapes = (
        jax.ShapeDtypeStruct((TENSOR, TOK, PART), both.dtype),
        jax.ShapeDtypeStruct((TENSOR, PIECE, LANES), both.dtype),
    )
    return kernel_call(split_kernel, shapes, (both,))


def example_grad_kernel(acts_ref, picked_ref, assign_ref, out_ref, spots_ref):
    blocks = [
        picked_ref[y * X : (y + 1) * X, j * TROWS : (j + 1) * TROWS].reshape(TOK, LANES)
        for y in range(Y_LO)
        for j in range(BLOCKS)
    ]
    picked = jnp.concatenate(blocks, axis=1)
    row = lax.broadcasted_iota(jnp.int32, (PART, NSEL), 0)
    lane = lax.broadcasted_iota(jnp.int32, (PART, NSEL), 1)
    spread = (row * NSEL + lane) * 40503
    count = PART // ROWS
    for t in range(TENSOR):
        grad = lax.dot_general(
            acts_ref[t], picked, (((0,), (0,)), ((), ())), preferred_element_type=jnp.float32
        )
        noise = jnp.bitwise_and(spread + t * 7919, 65535) * 128
        grad = pltpu.stochastic_round(grad, noise.astype(jnp.uint32), target_dtype=out_ref.dtype)
        out_ref[t * count : (t + 1) * count] = grad.reshape(count, ROWS, NSEL)
    column = lax.broadcasted_iota(jnp.int32, (SEQS, SEQS), 0)
    slot = lax.broadcasted_iota(jnp.int32, (SEQS, SEQS), 1)
    pair, core = column % PAIRS, column // PAIRS % CORES
    y_hi, place = column // (PAIRS * CORES) % Y_HI, column // (PAIRS * SIDES)
    ordered = jnp.where(batch_index(y_hi, pair, place, core) == slot, 1.0, 0.0)
    wanted = jnp.where(column == assign_ref[...], 1.0, 0.0)
    spots_ref[...] = lax.dot_general(
        ordered, wanted, (((1,), (1,)), ((), ())), preferred_element_type=jnp.float32
    )


def example_grad(acts, picked, assign):
    shapes = (
        jax.ShapeDtypeStruct((MEMBERS, ROWS, NSEL), acts.dtype),
        jax.ShapeDtypeStruct((SEQS, SEQS), jnp.float32),
    )
    return kernel_call(example_grad_kernel, shapes, (acts, picked, assign[None]))


def pairs_kernel(terms_ref, out_ref):
    terms = jnp.swapaxes(terms_ref[...], 0, 1)
    total = jnp.zeros((SEQS, SEQS), jnp.float32)
    for row in range(ROWS):
        total += lax.dot_general(
            terms[row], terms[row], (((1,), (1,)), ((), ())), preferred_element_type=jnp.float32
        )
    total = total * (1.0 / (float(TOK) * float(D) * float(NSEL)))
    for r in range(PLACES):
        for c in range(CORES):
            starts = [((r * Y_HI + y) * CORES + c) * PAIRS for y in range(Y_HI)]
            rows = [total[start : start + PAIRS] for start in starts]
            out_ref[:, r, c, 0] = jnp.concatenate(rows, axis=1)


def pairs(terms):
    shape = jax.ShapeDtypeStruct((PAIRS, PLACES, CORES, 1, Y_HI * SEQS), jnp.float32)
    return kernel_call(pairs_kernel, shape, (terms,))


def side_kernel(rows_ref, out_ref):
    sums = rows_ref[0]
    for member in range(1, DEPTH):
        sums = sums + rows_ref[member]
    for y in range(Y_HI):
        out_ref[y] = jnp.broadcast_to(sums[:, y * SEQS : (y + 1) * SEQS][None], (TENSOR, 1, SEQS))


def place_kernel(rows_ref, spots_ref, out_ref):
    row = rows_ref[0]
    for member in range(1, Y_HI * TENSOR):
        row = row + rows_ref[member]
    out_ref[...] = lax.dot_general(
        row,
        spots_ref[...],
        (((1,), (0,)), ((), ())),
        precision=lax.Precision.HIGHEST,
        preferred_element_type=jnp.float32,
    )


def on_device(acts, grads, chosen, assign):
    pair = (lax.axis_index("batch") // (PLACES * CORES) % PAIRS)[None]
    both = packed(pair, acts, selected(chosen, grads))
    both = lax.all_to_all(both, "tensor", 0, 0, tiled=True)
    part, copies = split(both)
    part = to_pair(part)
    picked = to_pair(lax.all_to_all(copies, "tensor", 0, 0, tiled=True))
    terms, spots = example_grad(part, picked, assign)
    terms = lax.all_to_all(
        terms, ("batch", "tensor"), 0, 0, axis_index_groups=pair_groups(), tiled=True
    )
    rows = pairs(terms).reshape(DEPTH, 1, Y_HI * SEQS)
    rows = lax.all_to_all(rows, "batch", 0, 0, axis_index_groups=depth_groups(), tiled=True)
    shape = jax.ShapeDtypeStruct((Y_HI, TENSOR, 1, SEQS), jnp.float32)
    rows = kernel_call(side_kernel, shape, (rows,)).reshape(Y_HI * TENSOR, 1, SEQS)
    rows = lax.all_to_all(
        rows, ("batch", "tensor"), 0, 0, axis_index_groups=side_groups(), tiled=True
    )
    shape = jax.ShapeDtypeStruct((1, SEQS), jnp.float32)
    return kernel_call(place_kernel, shape, (rows, spots))


def solution(mesh):
    placed = (P("batch", "tensor"), P("batch", "tensor"), P(), P())
    return jax.shard_map(
        on_device, mesh=mesh, in_specs=placed, out_specs=P("batch", None), check_vma=False
    )
```

```python
import jax
import jax.numpy as jnp
from jax import lax
from jax.experimental import pallas as pl
from jax.experimental.pallas import tpu as pltpu
from jax.sharding import PartitionSpec as P

D = 8192
NSEL = 512
TOK = 128
Y_HI, PAIRS, PLACES, CORES = 2, 8, 2, 2
SEQS = Y_HI * PAIRS * PLACES * CORES
SIDES = Y_HI * CORES
DEPTH = PAIRS * PLACES * CORES
Y_LO, X = 2, 4
TENSOR = Y_LO * X
WIDTH = D // TENSOR
PART = WIDTH // PAIRS
HALF = NSEL // Y_LO
TROWS = TOK // X
LANES = 128
BLOCKS = HALF // LANES
PIECE = BLOCKS * TROWS
MEMBERS = PLACES * SIDES * TENSOR
ROWS = WIDTH // MEMBERS
PAIR_OF = (
    (4, 1, 2, 7, 0, 5, 6, 3),
    (3, 7, 1, 5, 2, 6, 0, 4),
    (5, 0, 3, 6, 1, 4, 7, 2),
    (2, 6, 4, 1, 7, 3, 5, 0),
    (6, 2, 5, 0, 3, 7, 4, 1),
    (1, 4, 7, 2, 5, 0, 3, 6),
    (7, 3, 0, 4, 6, 2, 1, 5),
    (0, 5, 6, 3, 4, 1, 2, 7),
)


def batch_index(y_hi, pair, place, core):
    return ((y_hi * PAIRS + pair) * PLACES + place) * CORES + core


def place_of(t, k, place):
    return 1 - place if (PAIR_OF[t][k] - k) % PAIRS == PAIRS // 2 else place


def to_pair(block):
    route = [
        (
            batch_index(y, k, r, c) * TENSOR + t,
            batch_index(y, PAIR_OF[t][k], place_of(t, k, r), c) * TENSOR + t,
        )
        for y in range(Y_HI)
        for k in range(PAIRS)
        for r in range(PLACES)
        for c in range(CORES)
        for t in range(TENSOR)
    ]
    return lax.ppermute(block, ("batch", "tensor"), route)


def pair_groups():
    held_by = [
        [next(t for t in range(TENSOR) if PAIR_OF[t][k] == pair) for k in range(PAIRS)]
        for pair in range(PAIRS)
    ]
    return [
        [
            batch_index(y, pair, place_of(held_by[pair][k], k, r), c) * TENSOR + held_by[pair][k]
            for r in range(PLACES)
            for y in range(Y_HI)
            for c in range(CORES)
            for k in range(PAIRS)
        ]
        for pair in range(PAIRS)
    ]


def depth_groups():
    return [
        [batch_index(y, k, r, c) for k in range(PAIRS) for r in range(PLACES) for c in range(CORES)]
        for y in range(Y_HI)
    ]


def side_groups():
    return [
        [batch_index(y, k, r, c) * TENSOR + t for y in range(Y_HI) for t in range(TENSOR)]
        for k in range(PAIRS)
        for r in range(PLACES)
        for c in range(CORES)
    ]


def kernel_call(kernel, out_shape, args, scalars=()):
    smem = pl.BlockSpec(memory_space=pltpu.SMEM)
    vmem = pl.BlockSpec(memory_space=pltpu.VMEM)
    return pl.pallas_call(
        kernel,
        out_shape=out_shape,
        in_specs=[smem] * len(scalars) + [vmem] * len(args),
        out_specs=jax.tree.map(lambda _: vmem, out_shape),
        compiler_params=pltpu.CompilerParams(vmem_limit_bytes=24 * 1024 * 1024),
    )(*scalars, *args)


def chosen_by(number, values):
    found = values[0]
    for i in range(1, len(values)):
        found = jnp.where(number == i, values[i], found)
    return found


def selected(chosen, grads):
    local = chosen - lax.axis_index("tensor") * WIDTH
    places = lax.broadcasted_iota(jnp.int32, (WIDTH, NSEL), 0)
    selector = (places == local[None, :]).astype(grads.dtype)
    return lax.dot_general(
        grads, selector, (((1,), (0,)), ((), ())), preferred_element_type=jnp.float32
    ).astype(grads.dtype)


def pack_kernel(pair_ref, acts_ref, part_ref, out_ref):
    for t in range(TENSOR):
        start = pl.multiple_of(chosen_by(pair_ref[0], PAIR_OF[t]) * PART, PART)
        out_ref[t, :TOK] = acts_ref[:, pl.ds(start, PART)]
        y, x = t // X, t % X
        for j in range(BLOCKS):
            lane = (y * BLOCKS + j) * LANES
            block = part_ref[x * TROWS : (x + 1) * TROWS, lane : lane + LANES]
            out_ref[t, TOK + j * TROWS : TOK + (j + 1) * TROWS] = block


def packed(pair, acts, part):
    shape = jax.ShapeDtypeStruct((TENSOR, TOK + PIECE, LANES), acts.dtype)
    return kernel_call(pack_kernel, shape, (acts, part), (pair,))


def split_kernel(both_ref, acts_ref, copies_ref):
    acts_ref[...] = both_ref[:, :TOK]
    piece = both_ref[0, TOK:].astype(jnp.float32)
    for t in range(1, TENSOR):
        piece = piece + both_ref[t, TOK:].astype(jnp.float32)
    copies_ref[...] = jnp.broadcast_to(piece.astype(copies_ref.dtype)[None], copies_ref.shape)


def split(both):
    shapes = (
        jax.ShapeDtypeStruct((TENSOR, TOK, PART), both.dtype),
        jax.ShapeDtypeStruct((TENSOR, PIECE, LANES), both.dtype),
    )
    return kernel_call(split_kernel, shapes, (both,))


def example_grad_kernel(acts_ref, picked_ref, assign_ref, out_ref, spots_ref):
    blocks = [
        picked_ref[y * X : (y + 1) * X, j * TROWS : (j + 1) * TROWS].reshape(TOK, LANES)
        for y in range(Y_LO)
        for j in range(BLOCKS)
    ]
    picked = jnp.concatenate(blocks, axis=1)
    row = lax.broadcasted_iota(jnp.int32, (PART, NSEL), 0)
    lane = lax.broadcasted_iota(jnp.int32, (PART, NSEL), 1)
    spread = (row * NSEL + lane) * 40503
    count = PART // ROWS
    for t in range(TENSOR):
        grad = lax.dot_general(
            acts_ref[t], picked, (((0,), (0,)), ((), ())), preferred_element_type=jnp.float32
        )
        noise = jnp.bitwise_and(spread + t * 7919, 65535) * 128
        grad = pltpu.stochastic_round(grad, noise.astype(jnp.uint32), target_dtype=out_ref.dtype)
        out_ref[t * count : (t + 1) * count] = grad.reshape(count, ROWS, NSEL)
    column = lax.broadcasted_iota(jnp.int32, (SEQS, SEQS), 0)
    slot = lax.broadcasted_iota(jnp.int32, (SEQS, SEQS), 1)
    pair, core = column % PAIRS, column // PAIRS % CORES
    y_hi, place = column // (PAIRS * CORES) % Y_HI, column // (PAIRS * SIDES)
    ordered = jnp.where(batch_index(y_hi, pair, place, core) == slot, 1.0, 0.0)
    wanted = jnp.where(column == assign_ref[...], 1.0, 0.0)
    spots_ref[...] = lax.dot_general(
        ordered, wanted, (((1,), (1,)), ((), ())), preferred_element_type=jnp.float32
    )


def example_grad(acts, picked, assign):
    shapes = (
        jax.ShapeDtypeStruct((MEMBERS, ROWS, NSEL), acts.dtype),
        jax.ShapeDtypeStruct((SEQS, SEQS), jnp.float32),
    )
    return kernel_call(example_grad_kernel, shapes, (acts, picked, assign[None]))


def pairs_kernel(terms_ref, out_ref):
    terms = jnp.swapaxes(terms_ref[...], 0, 1)
    total = jnp.zeros((SEQS, SEQS), jnp.float32)
    for row in range(ROWS):
        total += lax.dot_general(
            terms[row], terms[row], (((1,), (1,)), ((), ())), preferred_element_type=jnp.float32
        )
    total = total * (1.0 / (float(TOK) * float(D) * float(NSEL)))
    for r in range(PLACES):
        for c in range(CORES):
            starts = [((r * Y_HI + y) * CORES + c) * PAIRS for y in range(Y_HI)]
            rows = [total[start : start + PAIRS] for start in starts]
            out_ref[:, r, c, 0] = jnp.concatenate(rows, axis=1)


def pairs(terms):
    shape = jax.ShapeDtypeStruct((PAIRS, PLACES, CORES, 1, Y_HI * SEQS), jnp.float32)
    return kernel_call(pairs_kernel, shape, (terms,))


def side_kernel(rows_ref, out_ref):
    sums = rows_ref[0]
    for member in range(1, DEPTH):
        sums = sums + rows_ref[member]
    for y in range(Y_HI):
        out_ref[y] = jnp.broadcast_to(sums[:, y * SEQS : (y + 1) * SEQS][None], (TENSOR, 1, SEQS))


def place_kernel(rows_ref, spots_ref, out_ref):
    row = rows_ref[0]
    for member in range(1, Y_HI * TENSOR):
        row = row + rows_ref[member]
    out_ref[...] = lax.dot_general(
        row,
        spots_ref[...],
        (((1,), (0,)), ((), ())),
        precision=lax.Precision.HIGHEST,
        preferred_element_type=jnp.float32,
    )


def on_device(acts, grads, chosen, assign):
    pair = (lax.axis_index("batch") // (PLACES * CORES) % PAIRS)[None]
    both = packed(pair, acts, selected(chosen, grads))
    both = lax.all_to_all(both, "tensor", 0, 0, tiled=True)
    part, copies = split(both)
    part = to_pair(part)
    picked = to_pair(lax.all_to_all(copies, "tensor", 0, 0, tiled=True))
    terms, spots = example_grad(part, picked, assign)
    terms = lax.all_to_all(
        terms, ("batch", "tensor"), 0, 0, axis_index_groups=pair_groups(), tiled=True
    )
    rows = pairs(terms).reshape(DEPTH, 1, Y_HI * SEQS)
    rows = lax.all_to_all(rows, "batch", 0, 0, axis_index_groups=depth_groups(), tiled=True)
    shape = jax.ShapeDtypeStruct((Y_HI, TENSOR, 1, SEQS), jnp.float32)
    rows = kernel_call(side_kernel, shape, (rows,)).reshape(Y_HI * TENSOR, 1, SEQS)
    rows = lax.all_to_all(
        rows, ("batch", "tensor"), 0, 0, axis_index_groups=side_groups(), tiled=True
    )
    shape = jax.ShapeDtypeStruct((1, SEQS), jnp.float32)
    return kernel_call(place_kernel, shape, (rows, spots))


def solution(mesh):
    placed = (P("batch", "tensor"), P("batch", "tensor"), P(), P())
    return jax.shard_map(
        on_device, mesh=mesh, in_specs=placed, out_specs=P("batch", None), check_vma=False
    )
```
